128 devices in a mesh: src: 8 (over x, core), tgt: 16 (over y, z).
Axes of the slice: x: 4, y: 4, z: 4, core: 2. Of those that a mesh axis runs over, the one named last changes fastest.
Arguments:
- source_points: float32 [3, 524288], P(None, ('src', 'tgt')), may hold values from 0 to 2
- source_values: bfloat16 [524288, 128], P(('src', 'tgt')), may hold values from -0.031982422 to 0.033935547
- leaf_index: int32 [1024, 512], P(('src', 'tgt')), may hold values from 0 to 4095, as said below
- leaf_pivots: int32 [1024, 256], P(('src', 'tgt')), may hold values from 0 to 511, as said below
- leaf_proj: bfloat16 [1024, 256, 512], P(('src', 'tgt')), may hold values from -0.25 to 0.25
- node_pivots: int32 [128, 256], P(('src', 'tgt')), may hold values from 0 to 2047, as said below
- node_proj: bfloat16 [128, 256, 2048], P(('src', 'tgt')), may hold values from -0.125 to 0.125
- top_pivots: int32 [16, 256], P('tgt'), may hold values from 0 to 2047, as said below
- top_proj: bfloat16 [16, 256, 2048], P('tgt', None, 'src'), may hold values from -0.125 to 0.125
- target_points: float32 [3, 65536], P(None, 'tgt'), may hold values from 0 to 2
- near_list: int32 [8, 256, 8], P('src', 'tgt'), may hold values from 0 to 23, as said below
- near_count: int32 [8, 256], P('src', 'tgt'), may hold values from 0 to 8, as said below
- far_list: int32 [8, 256, 12], P('src', 'tgt'), may hold values from 0 to 23, as said below
- far_count: int32 [8, 256], P('src', 'tgt'), may hold values from 0 to 12, as said below
- node_list: int32 [8, 256, 4], P('src', 'tgt'), may hold values from 0 to 15, as said below
- node_count: int32 [8, 256], P('src', 'tgt'), may hold values from 0 to 4, as said below
- top_list: int32 [256, 12], P('tgt'), may hold values from 0 to 15, as said below
- top_count: int32 [256], P('tgt'), may hold values from 1 to 12, as said below
Outputs:
- posterior: float32 [65536, 128], P('tgt', 'src')
The draws below stay inside these ranges and needn't reach their ends.
Inputs may be any that keep to these rules, and one draw needn't show every extreme that they name: `leaf_index`: each block of 8 rows (one node) holds every number of 0 to 4095 once. `leaf_pivots`: entries of a row are distinct. `node_pivots`: entries of a row are distinct. `top_pivots`: entries of a row are distinct. `near_list`: entries of a row are distinct and differ from those of far_list in the same row. `far_list`: entries of a row are distinct. `near_count`: zero for target leaves whose block differs from i by more than one; in each block and column some target leaf reaches 8. `far_count`: zero for target leaves whose block differs from i by more than one; in each block and column some target leaf reaches 12. `node_list`: entries of a row are distinct. `node_count`: zero for target leaves whose block differs from i by at most one; in each block and column some target leaf reaches 4. `top_list`: entries of a row are distinct. `top_count`: in each column some target leaf reaches 12.
All inputs are finite; a program needn't handle non-finite values.
Results may differ from the reference program's by a relative error of at most 0.0075.
Values may be sent and summed in bfloat16 or wider, within the bound.
No kernel may reach another device: no remote copies, remote signals or barrier semaphores. Data moves between devices by JAX's collectives and lax.ppermute only.
A program may use at most 64 MiB of HBM per device.

```python
import jax
import jax.numpy as jnp
from jax import lax

LEAF = 512
SKEL = 256
Q = 128
SL = 8
TLEAF = 256
TLX = 2
NEAR_MAX = 8
LFAR_MAX = 12
N1_MAX = 4
N2_MAX = 12
TL_J = 16
NTL = 256
NT = 65536
NODES = 128
NSL = 1024
NS = 524288
N_SRC = 8
N_TGT = 16


def row_perms(key, rows, total, keep):
    keys = jax.random.split(key, rows)
    return jax.vmap(lambda single: jax.random.permutation(single, total)[:keep])(keys).astype(jnp.int32)


def halo_lists(key):
    picks = row_perms(jax.random.fold_in(key, 50), N_SRC * NTL, 3 * SL, NEAR_MAX + LFAR_MAX)
    return picks.reshape(N_SRC, NTL, NEAR_MAX + LFAR_MAX)


def ragged_counts(key, most, near_zone, chosen_block):
    first, second = jax.random.split(key)
    counts = jax.random.randint(first, (N_SRC, NTL), 1, most + 1).astype(jnp.int32)
    within = jax.random.randint(second, (N_SRC, N_TGT), 0, TLX).astype(jnp.int32)
    forced = chosen_block[:, None] * TLX + within
    leaves = jnp.arange(NTL, dtype=jnp.int32)
    local = leaves % TL_J
    column = leaves // TL_J
    hit = local[None, :] == forced[:, column]
    blocks = jnp.arange(N_SRC, dtype=jnp.int32)[:, None]
    distance = jnp.abs(local[None, :] // TLX - blocks)
    zone = distance <= 1 if near_zone else distance > 1
    return jnp.where(zone, jnp.where(hit, most, counts), 0).astype(jnp.int32)


def draw_leaf_index(key, part):
    key = jax.random.fold_in(key, 1)
    return row_perms(key, NODES, SL * LEAF, SL * LEAF).reshape(NSL, LEAF)


def draw_leaf_pivots(key, part):
    key = jax.random.fold_in(key, 2)
    return row_perms(key, NSL, LEAF, SKEL)


def draw_node_pivots(key, part):
    key = jax.random.fold_in(key, 3)
    return row_perms(key, NODES, SL * SKEL, SKEL)


def draw_top_pivots(key, part):
    key = jax.random.fold_in(key, 4)
    return row_perms(key, N_TGT, N_SRC * SKEL, SKEL)


def draw_near_list(key, part):
    return halo_lists(key)[:, :, :NEAR_MAX]


def draw_far_list(key, part):
    return halo_lists(key)[:, :, NEAR_MAX:]


def draw_near_count(key, part):
    key = jax.random.fold_in(key, 5)
    return ragged_counts(key, NEAR_MAX, True, jnp.arange(N_SRC, dtype=jnp.int32))


def draw_far_count(key, part):
    key = jax.random.fold_in(key, 6)
    return ragged_counts(key, LFAR_MAX, True, jnp.arange(N_SRC, dtype=jnp.int32))


def draw_node_count(key, part):
    key = jax.random.fold_in(key, 7)
    first, second = jax.random.split(key)
    shift = jax.random.randint(first, (N_SRC,), 0, N_SRC - 3).astype(jnp.int32)
    chosen = (jnp.arange(N_SRC, dtype=jnp.int32) + 2 + shift) % N_SRC
    return ragged_counts(second, N1_MAX, False, chosen)


def draw_node_list(key, part):
    key = jax.random.fold_in(key, 8)
    return row_perms(key, N_SRC * NTL, N_TGT, N1_MAX).reshape(N_SRC, NTL, N1_MAX)


def draw_top_list(key, part):
    key = jax.random.fold_in(key, 9)
    return row_perms(key, NTL, N_TGT, N2_MAX)


def draw_top_count(key, part):
    key = jax.random.fold_in(key, 10)
    first, second = jax.random.split(key)
    counts = jax.random.randint(first, (NTL,), 1, N2_MAX + 1).astype(jnp.int32)
    forced = jax.random.randint(second, (N_TGT,), 0, TL_J).astype(jnp.int32)
    leaves = jnp.arange(NTL, dtype=jnp.int32)
    hit = leaves % TL_J == forced[leaves // TL_J]
    return jnp.where(hit, N2_MAX, counts).astype(jnp.int32)


def block_scale(key, dims, pieces, least, top_value):
    factor_of, own = 1.0, jax.random.fold_in(key, 6)
    for dim, shards_of in pieces:
        draws = jnp.exp(jax.random.uniform(jax.random.fold_in(own, dim), (shards_of,), jnp.float32, least / len(pieces), top_value / len(pieces)))
        factor_of = factor_of * jnp.repeat(draws, dims[dim] // shards_of).reshape([-1 if axis == dim else 1 for axis in range(len(dims))])
    return factor_of


def centred(rng, shape, width, bound, cuts=(), held_as=jnp.bfloat16):
    drawn = jax.random.normal(rng, shape, jnp.float32) * width
    if len(cuts) > 0:
        drawn = block_scale(rng, shape, cuts, -0.22, 0.18) * drawn
    return jnp.clip(drawn, min=-bound, max=bound).astype(held_as)


def setup_inputs(seed: int = 0) -> dict:
    seeds = jax.random.split(jax.random.key(seed), 19)
    return {
        "source_points": jnp.clip(2.0 * jax.random.uniform(seeds[0], (3, NS), jnp.float32) ** block_scale(seeds[0], (3, NS), ((1, 128),), -0.2, 0.2), 0.0, 2.0),
        "source_values": jnp.clip(-0.031982422 + 0.06591797 * jax.random.uniform(seeds[1], (NS, Q), jnp.float32) ** block_scale(seeds[1], (NS, Q), ((0, 128),), -0.2, 0.2), -0.031982422, 0.033935547).astype(jnp.bfloat16),
        "leaf_index": draw_leaf_index(jax.random.fold_in(seeds[18], 71), 0),
        "leaf_pivots": draw_leaf_pivots(jax.random.fold_in(seeds[18], 71), 0),
        "leaf_proj": centred(seeds[4], (NSL, SKEL, LEAF), LEAF ** -0.5, 0.25, ((0, 128),)),
        "node_pivots": draw_node_pivots(jax.random.fold_in(seeds[18], 71), 0),
        "node_proj": centred(seeds[6], (NODES, SKEL, SL * SKEL), (SL * SKEL) ** -0.5, 0.125, ((0, 128),)),
        "top_pivots": draw_top_pivots(jax.random.fold_in(seeds[18], 71), 0),
        "top_proj": centred(seeds[8], (N_TGT, SKEL, N_SRC * SKEL), (N_SRC * SKEL) ** -0.5, 0.125, ((0, 16), (2, 8))),
        "target_points": jnp.clip(2.0 * jax.random.uniform(seeds[9], (3, NT), jnp.float32) ** block_scale(seeds[9], (3, NT), ((1, 16),), -0.2, 0.2), 0.0, 2.0),
        "near_list": draw_near_list(jax.random.fold_in(seeds[18], 71), 0),
        "near_count": draw_near_count(jax.random.fold_in(seeds[18], 71), 0),
        "far_list": draw_far_list(jax.random.fold_in(seeds[18], 71), 0),
        "far_count": draw_far_count(jax.random.fold_in(seeds[18], 71), 0),
        "node_list": draw_node_list(jax.random.fold_in(seeds[18], 71), 0),
        "node_count": draw_node_count(jax.random.fold_in(seeds[18], 71), 0),
        "top_list": draw_top_list(jax.random.fold_in(seeds[18], 71), 0),
        "top_count": draw_top_count(jax.random.fold_in(seeds[18], 71), 0),
    }


rate = 2.0
pair_group = 8

def matern(targets, points):
    diff = targets[..., :, :, None] - points[..., :, None, :]
    dist = jnp.sqrt(lax.optimization_barrier(jnp.sum(diff * diff, axis=-3)))
    scaled = rate * dist
    return (1.0 + scaled) * jnp.exp(-scaled)

def alive_mask(counts, breadth):
    return jnp.arange(breadth, dtype=jnp.int32)[None, :] < counts[:, None]

def listed_sums(targets, lists, alive, points, values):
    leaves, breadth = lists.shape
    flat_alive = alive.reshape(-1)
    ordered = jnp.argsort(jnp.where(flat_alive, 0, 1).astype(jnp.int32), stable=True).astype(jnp.int32)
    ordered = jnp.concatenate([ordered, jnp.zeros((pair_group,), jnp.int32)])
    total_live = jnp.sum(flat_alive.astype(jnp.int32))
    turns = (total_live + pair_group - 1) // pair_group
    offsets = jnp.arange(pair_group, dtype=jnp.int32)

    def advance(number, accum):
        pair_ids = lax.dynamic_slice_in_dim(ordered, number * pair_group, pair_group)
        usable = number * pair_group + offsets < total_live
        leaf_of = pair_ids // breadth
        source_ids = lists[leaf_of, pair_ids % breadth]
        kernel = matern(targets[leaf_of], points[source_ids])
        kernel = jnp.where(usable[:, None, None], kernel, 0.0).astype(jnp.bfloat16)
        result = jnp.einsum('gam,gmq->gaq', kernel.astype(jnp.float32), values[source_ids].astype(jnp.float32))
        return accum.at[leaf_of].add(result)
    start = jnp.zeros((leaves, targets.shape[2], values.shape[2]), jnp.float32)
    return lax.fori_loop(0, turns, advance, start)

def block_data(member):
    points, values, index, pivots, proj, npiv, nproj = member
    leaf_vals = values[index]
    leaf_pts = jnp.transpose(points[:, index], (1, 0, 2))
    skel_pts = jnp.take_along_axis(leaf_pts, jnp.broadcast_to(pivots[:, None, :], (SL, 3, SKEL)), axis=2)
    skel_vals = jnp.einsum('lsm,lmq->lsq', proj.astype(jnp.float32), leaf_vals.astype(jnp.float32)).astype(jnp.bfloat16)
    node_vals = jnp.dot(nproj, skel_vals.reshape(SL * SKEL, Q), preferred_element_type=jnp.float32).astype(jnp.bfloat16)
    child_pts = jnp.transpose(skel_pts, (1, 0, 2)).reshape(3, SL * SKEL)
    node_pts = child_pts[:, npiv]
    return (jnp.concatenate([leaf_vals, skel_vals], axis=1), jnp.concatenate([leaf_pts, skel_pts], axis=2), node_vals, node_pts)

def reference(source_points, source_values, leaf_index, leaf_pivots, leaf_proj, node_pivots, node_proj, top_pivots, top_proj, target_points, near_list, near_count, far_list, far_count, node_list, node_count, top_list, top_count):
    blocks = N_SRC * N_TGT
    pts_b = jnp.transpose(source_points.reshape(3, blocks, SL * LEAF), (1, 0, 2))
    vals_b = source_values.reshape(blocks, SL * LEAF, Q)
    halo_vals, halo_pts, node_vals, node_pts = lax.map(block_data, (pts_b, vals_b, leaf_index.reshape(blocks, SL, LEAF), leaf_pivots.reshape(blocks, SL, SKEL), leaf_proj.reshape(blocks, SL, SKEL, LEAF), node_pivots, node_proj))
    halo_vals = halo_vals.reshape(N_SRC, N_TGT, SL, LEAF + SKEL, Q)
    halo_pts = halo_pts.reshape(N_SRC, N_TGT, SL, 3, LEAF + SKEL)
    node_vals = node_vals.reshape(N_SRC, N_TGT, SKEL, Q)
    node_pts = node_pts.reshape(N_SRC, N_TGT, 3, SKEL)
    padded_vals = jnp.pad(halo_vals, ((0, 0), (1, 1), (0, 0), (0, 0), (0, 0)))
    padded_pts = jnp.pad(halo_pts, ((0, 0), (1, 1), (0, 0), (0, 0), (0, 0)))
    children = jnp.transpose(node_vals, (1, 0, 2, 3)).reshape(N_TGT, N_SRC * SKEL, Q)
    top_vals = jnp.einsum('jsc,jcq->jsq', top_proj.astype(jnp.float32), children.astype(jnp.float32)).astype(jnp.bfloat16)
    children_pts = jnp.transpose(node_pts, (1, 2, 0, 3)).reshape(N_TGT, 3, N_SRC * SKEL)
    top_pts = jnp.take_along_axis(children_pts, jnp.broadcast_to(top_pivots[:, None, :], (N_TGT, 3, SKEL)), axis=2)
    targets_all = jnp.transpose(target_points.reshape(3, N_TGT, TL_J, TLEAF), (1, 2, 0, 3))
    near_l = near_list.reshape(N_SRC, N_TGT, TL_J, NEAR_MAX)
    near_c = near_count.reshape(N_SRC, N_TGT, TL_J)
    far_l = far_list.reshape(N_SRC, N_TGT, TL_J, LFAR_MAX)
    far_c = far_count.reshape(N_SRC, N_TGT, TL_J)
    node_l = node_list.reshape(N_SRC, N_TGT, TL_J, N1_MAX)
    node_c = node_count.reshape(N_SRC, N_TGT, TL_J)
    top_l = top_list.reshape(N_TGT, TL_J, N2_MAX)
    top_c = top_count.reshape(N_TGT, TL_J)

    def column_sum(column):
        column_tgts = targets_all[column]

        def source_block(block, accum):
            halo_v = lax.dynamic_slice_in_dim(padded_vals[block], column, 3, 0).reshape(3 * SL, LEAF + SKEL, Q)
            halo_p = lax.dynamic_slice_in_dim(padded_pts[block], column, 3, 0).reshape(3 * SL, 3, LEAF + SKEL)
            near = listed_sums(column_tgts, near_l[block, column], alive_mask(near_c[block, column], NEAR_MAX), halo_p[:, :, :LEAF], halo_v[:, :LEAF])
            far = listed_sums(column_tgts, far_l[block, column], alive_mask(far_c[block, column], LFAR_MAX), halo_p[:, :, LEAF:], halo_v[:, LEAF:])
            nodes = listed_sums(column_tgts, node_l[block, column], alive_mask(node_c[block, column], N1_MAX), node_pts[block], node_vals[block])
            partial_value = near + far + nodes
            start = block * TLX
            top_rows = listed_sums(lax.dynamic_slice_in_dim(column_tgts, start, TLX, 0), lax.dynamic_slice_in_dim(top_l[column], start, TLX, 0), alive_mask(lax.dynamic_slice_in_dim(top_c[column], start, TLX, 0), N2_MAX), top_pts, top_vals)
            current = lax.dynamic_slice_in_dim(partial_value, start, TLX, 0)
            partial_value = lax.dynamic_update_slice_in_dim(partial_value, current + top_rows, start, 0)
            return accum + partial_value
        return lax.fori_loop(0, N_SRC, source_block, jnp.zeros((TL_J, TLEAF, Q), jnp.float32))
    means = lax.map(column_sum, jnp.arange(N_TGT, dtype=jnp.int32))
    return means.reshape(NT, Q)
```

```python
import functools

import jax
import jax.numpy as jnp
from jax import lax
from jax.experimental import pallas as pl
from jax.experimental.pallas import tpu as pltpu
from jax.sharding import PartitionSpec as P

SL = 8
LEAF = 512
SKEL = 256
Q = 128
TLEAF = 256
TL_J = 16
WIN = 6
KF = 16
LN2 = 0.6931471805599453
SCALE = 2.0 / LN2
GROUP = 16
VMEM = pltpu.VMEM
SMEM = pltpu.SMEM
bf16 = jnp.bfloat16
f32 = jnp.float32
NEAR_AT, FAR_AT, NODE_AT, TOP_AT = 0, 8, 20, 24
NEAR_N, FAR_N, NODE_N, TOP_N = 36, 37, 38, 39
TRASH = 16


def split2(x):
    high = x.astype(bf16).astype(f32)
    return high, (x - high).astype(bf16).astype(f32)


def split3(x):
    high, rest = split2(x)
    return high, rest, (x - high - rest).astype(bf16).astype(f32)


def centred(x):
    return (x - 1.0) * SCALE


def features(coords, is_source):
    pieces = [split2(c) for c in coords]
    high = [p[0] for p in pieces]
    low = [p[1] for p in pieces]
    norm = sum((h + r) * (h + r) for h, r in pieces)
    norms = list(split3(norm))
    one = jnp.ones_like(norm)
    zero = jnp.zeros_like(norm)
    if is_source:
        high = [-2.0 * h for h in high]
        low = [-2.0 * r for r in low]
        return high + low + high + [one, one, one] + norms + [zero]
    return high + high + low + norms + [one, one, one] + [zero]


def matern(w):
    w = jnp.maximum(w, 1e-12)
    u = w * lax.rsqrt(w)
    return ((1.0 + LN2 * u) * jnp.exp2(-u)).astype(bf16)


def take(row, index):
    return jnp.take_along_axis(row, index, axis=1, mode="promise_in_bounds")


def pick(chunks, index):
    low = index & 127
    high = index >> 7
    result = jnp.zeros((8, 128), f32)
    for k, chunk in enumerate(chunks):
        result = jnp.where(high == k, take(chunk, low), result)
    return result


def lanes(x, m):
    return x[:, 128 * m : 128 * (m + 1)]


def leaf_kernel(
    meta, idx_s, idx, piv, npiv, tpiv, pts, vals, proj, nproj, tproj,
    v_out, f_out, n_out, t_out, wide, gathered, fs, ns,
):
    src, chip, core = meta[0], meta[1], meta[2]
    rows = vals.shape[0]

    def widen(k, _):
        at = pl.multiple_of(k * 512, 512)
        wide[pl.ds(at, 512), :] = vals[pl.ds(at, 512), :].astype(f32)
        return 0

    lax.fori_loop(0, rows // 512, widen, 0)

    def gather(k, _):
        leaf = k // 16
        base = (k % 16) * 32
        at = pl.multiple_of(k * 32, 32)
        for r in range(32):
            gathered[pl.ds(at + r, 1), :] = wide[pl.ds(idx_s[leaf, base + r], 1), :]
        return 0

    lax.fori_loop(0, rows // 32, gather, 0)

    for leaf in range(SL):
        leaf_vals = gathered[leaf * LEAF : (leaf + 1) * LEAF, :].astype(bf16)
        v_out[2 * leaf] = leaf_vals[:256]
        v_out[2 * leaf + 1] = leaf_vals[256:]
        v_out[16 + leaf] = jnp.dot(proj[leaf], leaf_vals, preferred_element_type=f32).astype(bf16)
    node_vals = jnp.dot(
        nproj[0], v_out[16:24].reshape(SL * SKEL, Q), preferred_element_type=f32
    ).astype(bf16)
    n_out[0:256, :] = node_vals
    top = jnp.dot(tproj[0], node_vals, preferred_element_type=f32).T

    index = idx[...]
    pivots = piv[...]
    node_piv = jnp.broadcast_to(npiv[...], (8, SKEL))
    top_piv = jnp.broadcast_to(tpiv[...], (8, SKEL))
    leaf_of = lax.broadcasted_iota(jnp.int32, (8, 128), 0)
    leaf_c, skel_c, node_c, top_c = [], [], [], []
    for c in range(3):
        chunks = [jnp.broadcast_to(pts[c : c + 1, 128 * k : 128 * (k + 1)], (8, 128)) for k in range(rows // 128)]
        leaf_x = [pick(chunks, lanes(index, m)) for m in range(4)]
        skel_x = [pick(leaf_x, lanes(pivots, m)) for m in range(2)]
        node_x = []
        top_x = []
        for m in range(2):
            at = lanes(node_piv, m)
            mine = jnp.where(leaf_of == (at >> 8), pick(skel_x, at & 255), 0.0)
            node_x.append(jnp.broadcast_to(jnp.sum(mine, axis=0, keepdims=True), (8, 128)))
        for m in range(2):
            at = lanes(top_piv, m)
            top_x.append(jnp.where((at >> 8) == src, centred(pick(node_x, at & 255)), 0.0))
        leaf_c.append(centred(jnp.concatenate(leaf_x, axis=1)))
        skel_c.append(centred(jnp.concatenate(skel_x, axis=1)))
        node_c.append(centred(jnp.concatenate(node_x, axis=1)))
        top_c.append(jnp.concatenate(top_x, axis=1))
    for f, (a, b, n) in enumerate(zip(features(leaf_c, True), features(skel_c, True), features(node_c, True))):
        for leaf in range(SL):
            fs[2 * leaf, f : f + 1, :] = a[leaf : leaf + 1, :256]
            fs[2 * leaf + 1, f : f + 1, :] = a[leaf : leaf + 1, 256:]
            fs[16 + leaf, f : f + 1, :] = b[leaf : leaf + 1, :]
        ns[f : f + 1, :] = n[0:1, :]
    f_out[...] = fs[...].astype(bf16)
    n_out[256:272, :] = ns[:, :128].astype(bf16)
    n_out[272:288, :] = ns[:, 128:].astype(bf16)
    ns[...] = jnp.zeros_like(ns)
    for c in range(3):
        for k, piece in enumerate(split3(top_c[c])):
            ns[3 * c + k : 3 * c + k + 1, :] = piece[0:1, :]
    pieces = ns[...].astype(bf16)
    for half in range(2):
        for x in range(4):
            for k in range(2):
                part = top[16 * (2 * x + k) : 16 * (2 * x + k) + 16, 128 * half : 128 * half + 128]
                at = (k ^ core, (x - chip) & 3)
                t_out[at[0], at[1], 32 * half : 32 * half + 16, :] = part.astype(bf16)
                t_out[at[0], at[1], 32 * half + 16 : 32 * half + 32, :] = lanes(pieces, half)


def target_rows(pts, fa):
    rows = features([centred(pts[c : c + 1, :]) for c in range(3)], False)
    for f, row in enumerate(rows):
        fa[f : f + 1, :] = row


def pad_pairs(ps, pt, n, trash):
    for r in range(GROUP):
        ps[n + r] = 0
        pt[n + r] = trash
    return (n + GROUP - 1) // GROUP


def run_pairs(ps, pt, turns, a_ref, f_ref, v_ref, acc):
    def step(g, _):
        for q in range(GROUP):
            s = ps[g * GROUP + q]
            t = pt[g * GROUP + q]
            w = jnp.dot(a_ref[t], f_ref[s], preferred_element_type=f32)
            acc[t] += jnp.dot(matern(w), v_ref[s], preferred_element_type=f32)
        return 0

    lax.fori_loop(0, turns, step, 0)


def leaf_pairs(ps, pt, n, lists, start, slot, base):
    def target(t, n):
        leaf = start + t

        def near(e, n):
            v = lists[leaf, NEAR_AT + e] - base
            ps[n] = 2 * v
            pt[n] = slot + t
            ps[n + 1] = 2 * v + 1
            pt[n + 1] = slot + t
            return n + jnp.where((v >= 0) & (v < SL), 2, 0)

        def far(e, n):
            v = lists[leaf, FAR_AT + e] - base
            ps[n] = 16 + v
            pt[n] = slot + t
            return n + jnp.where((v >= 0) & (v < SL), 1, 0)

        n = lax.fori_loop(0, lists[leaf, NEAR_N], near, n)
        return lax.fori_loop(0, lists[leaf, FAR_N], far, n)

    return lax.fori_loop(0, WIN, target, n)


def set_targets(fa, a_ref, start, slot):
    def one(t, _):
        at = pl.multiple_of((start + t) * TLEAF, TLEAF)
        a_ref[slot + t] = fa[:, pl.ds(at, TLEAF)].T.astype(bf16)
        return 0

    return one


def clear(acc):
    def one(t, _):
        acc[t] = jnp.zeros(acc.shape[1:], f32)
        return 0

    lax.fori_loop(0, acc.shape[0], one, 0)


def halo_kernel(meta, lists_l, lists_r, pts_l, pts_r, v_ref, f_ref, out_l, out_r, fa, a_ref, acc, ps, pt):
    start = meta[6]
    clear(acc)
    target_rows(pts_l, fa)
    lax.fori_loop(0, WIN, set_targets(fa, a_ref, start, 0), 0)
    target_rows(pts_r, fa)
    lax.fori_loop(0, WIN, set_targets(fa, a_ref, start, WIN), 0)
    a_ref[2 * WIN] = jnp.zeros((TLEAF, KF), bf16)
    n = leaf_pairs(ps, pt, 0, lists_l, start, 0, 16)
    n = leaf_pairs(ps, pt, n, lists_r, start, WIN, 0)
    run_pairs(ps, pt, pad_pairs(ps, pt, n, 2 * WIN), a_ref, f_ref, v_ref, acc)
    for t in range(WIN):
        out_l[t * TLEAF : (t + 1) * TLEAF, :] = acc[t].astype(bf16)
        out_r[t * TLEAF : (t + 1) * TLEAF, :] = acc[WIN + t].astype(bf16)


def own_kernel(meta, lists, pts, v_ref, f_ref, out, fa, a_ref, acc, ps, pt):
    start = meta[6]
    clear(acc)
    target_rows(pts, fa)
    lax.fori_loop(0, WIN, set_targets(fa, a_ref, start, 0), 0)
    a_ref[WIN] = jnp.zeros((TLEAF, KF), bf16)
    n = leaf_pairs(ps, pt, 0, lists, start, 0, 8)
    run_pairs(ps, pt, pad_pairs(ps, pt, n, WIN), a_ref, f_ref, v_ref, acc)
    for t in range(WIN):
        out[t] = acc[t]


def listed_pairs(ps, pt, lists, first, count_at, row, plane):
    def target(t, n):
        def one(e, n):
            column = lists[t, first + e]
            dr = (row - (column >> 2)) & 3
            dp = (plane - (column & 3)) & 3
            ps[n] = 4 * dr + dp
            pt[n] = t
            return n + 1

        return lax.fori_loop(0, lists[t, count_at], one, n)

    return lax.fori_loop(0, TL_J, target, 0)


def node_kernel(
    meta, lists, pts, own, halo_l, halo_r, y0, y1, y2, y3,
    out, fa, a_ref, acc, ys, f_ref, v_ref, ps, pt, sems,
):
    core, chip, row, plane, start = meta[2], meta[1], meta[4], meta[5], meta[6]
    copies = [pltpu.make_async_copy(y, ys.at[k], sems.at[k]) for k, y in enumerate((y0, y1, y2, y3))]
    for copy in copies:
        copy.start()
    clear(acc)
    for t in range(WIN):
        sides = halo_l[t * TLEAF : (t + 1) * TLEAF, :].astype(f32) + halo_r[t * TLEAF : (t + 1) * TLEAF, :].astype(f32)
        acc[start + t] = own[t] + sides
    target_rows(pts, fa)
    lax.fori_loop(0, TL_J, set_targets(fa, a_ref, 0, 0), 0)
    a_ref[TRASH] = jnp.zeros((TLEAF, KF), bf16)
    n = listed_pairs(ps, pt, lists, NODE_AT, NODE_N, row, plane)
    turns = pad_pairs(ps, pt, n, TRASH)
    for copy in copies:
        copy.wait()
    for k in range(4):
        for z in range(4):
            v_ref[4 * k + z] = ys[k, z * 288 : z * 288 + 256, :]
            f_ref[4 * k + z, :, 0:128] = ys[k, z * 288 + 256 : z * 288 + 272, :]
            f_ref[4 * k + z, :, 128:256] = ys[k, z * 288 + 272 : z * 288 + 288, :]
    run_pairs(ps, pt, turns, a_ref, f_ref, v_ref, acc)

    def turn(t, _):
        at = pl.multiple_of(t * TLEAF, TLEAF)
        block = acc[t].T.astype(bf16)
        for x in range(4):
            for k in range(2):
                begin = 16 * (2 * x + k)
                out[k ^ core, (x - chip) & 3, :, pl.ds(at, TLEAF)] = block[begin : begin + 16]
        return 0

    lax.fori_loop(0, TL_J, turn, 0)


def top_kernel(meta, lists, pts, tops, out, fa, a_ref, acc, f_ref, v_ref, fw, ps, pt):
    row, plane = meta[4], meta[5]
    clear(acc)
    target_rows(pts, fa)
    lax.fori_loop(0, TL_J, set_targets(fa, a_ref, 0, 0), 0)
    a_ref[TRASH] = jnp.zeros((TLEAF, KF), bf16)
    n = listed_pairs(ps, pt, lists, TOP_AT, TOP_N, row, plane)
    turns = pad_pairs(ps, pt, n, TRASH)
    for dz in range(4):
        for dy in range(4):
            slot = 4 * dy + dz
            base = (dz * 4 + dy) * 64
            for half in range(2):
                at = base + 32 * half
                vals = tops[at : at + 16, :].astype(f32)
                v_ref[slot, 128 * half : 128 * half + 128, :] = vals.T.astype(bf16)
                pieces = tops[at + 16 : at + 32, :].astype(f32)
                coords = [
                    pieces[3 * c : 3 * c + 1] + pieces[3 * c + 1 : 3 * c + 2] + pieces[3 * c + 2 : 3 * c + 3]
                    for c in range(3)
                ]
                for f, line in enumerate(features(coords, True)):
                    fw[f : f + 1, 128 * half : 128 * half + 128] = line
            f_ref[slot] = fw[...].astype(bf16)
    run_pairs(ps, pt, turns, a_ref, f_ref, v_ref, acc)

    def turn(t, _):
        at = pl.multiple_of(t * TLEAF, TLEAF)
        out[:, pl.ds(at, TLEAF)] = acc[t].T
        return 0

    lax.fori_loop(0, TL_J, turn, 0)


def whole(count):
    return [pl.BlockSpec(memory_space=VMEM)] * count


def params(mebibytes):
    return pltpu.CompilerParams(vmem_limit_bytes=mebibytes << 20)


def cost(flops, moved):
    return pl.CostEstimate(flops=int(flops), bytes_accessed=int(moved), transcendentals=0)


def pair_scratch():
    return [pltpu.SMEM((512,), jnp.int32), pltpu.SMEM((512,), jnp.int32)]


def shift(axis, count, fn):
    return [(i, fn(i)) for i in range(count) if 0 <= fn(i) < count]


def shards(
    source_points, source_values, leaf_index, leaf_pivots, leaf_proj, node_pivots, node_proj,
    top_pivots, top_proj, target_points, near_list, near_count, far_list, far_count,
    node_list, node_count, top_list, top_count,
):
    src = lax.axis_index("src")
    tgt = lax.axis_index("tgt")
    start = jnp.clip(2 * src - 2, 0, TL_J - WIN)
    meta = jnp.stack([src, src // 2, src % 2, tgt, tgt // 4, tgt % 4, start, src * 0]).astype(jnp.int32)
    lists = jnp.concatenate(
        [near_list[0], far_list[0], node_list[0], top_list, near_count[0][:, None], far_count[0][:, None],
         node_count[0][:, None], top_count[:, None]], axis=1)
    forward = shift("tgt", 16, lambda i: i + 1)
    backward = shift("tgt", 16, lambda i: i - 1)
    pts_l = lax.ppermute(target_points, "tgt", forward)
    pts_r = lax.ppermute(target_points, "tgt", backward)
    lists_l = lax.ppermute(lists, "tgt", forward)
    lists_r = lax.ppermute(lists, "tgt", backward)

    smem = pl.BlockSpec(memory_space=SMEM)
    v_all, f_all, node_own, top_own = pl.pallas_call(
        leaf_kernel,
        out_shape=(
            jax.ShapeDtypeStruct((24, 256, Q), bf16),
            jax.ShapeDtypeStruct((24, KF, 256), bf16),
            jax.ShapeDtypeStruct((288, Q), bf16),
            jax.ShapeDtypeStruct((2, 4, 64, 128), bf16),
        ),
        in_specs=[smem, smem] + whole(9),
        out_specs=tuple(whole(4)),
        scratch_shapes=[
            VMEM((4096, Q), f32),
            VMEM((4096, Q), f32),
            VMEM((24, KF, 256), f32),
            VMEM((KF, 256), f32),
        ],
        compiler_params=params(40),
        cost_estimate=cost(2 * 8e6, 8e6),
        name="leaf_stage",
    )(meta, leaf_index, leaf_index, leaf_pivots, node_pivots, top_pivots, source_points, source_values,
      leaf_proj, node_proj, top_proj)

    zshift = [shift("tgt", 16, lambda i, d=d: (i // 4) * 4 + (i % 4 + d) % 4) for d in range(4)]
    yshift = [shift("tgt", 16, lambda i, d=d: ((i // 4 + d) % 4) * 4 + i % 4) for d in range(4)]
    xshift = [shift("src", 8, lambda i, d=d: (i + 2 * d) % 8) for d in range(4)]
    cores = shift("src", 8, lambda i: i ^ 1)

    top_pair = top_own[0] + lax.ppermute(top_own[1], "src", cores)
    node_z = [node_own] + [lax.ppermute(node_own, "tgt", zshift[d]) for d in (1, 2, 3)]
    top_sum = top_pair[0].astype(f32)
    for d in (1, 2, 3):
        top_sum = top_sum + lax.ppermute(top_pair[d], "src", xshift[d]).astype(f32)
    top_sum = top_sum.astype(bf16)

    halo_l, halo_r = pl.pallas_call(
        halo_kernel,
        out_shape=(jax.ShapeDtypeStruct((WIN * TLEAF, Q), bf16),) * 2,
        in_specs=[smem, smem, smem] + whole(4),
        out_specs=tuple(whole(2)),
        scratch_shapes=[
            VMEM((KF, TL_J * TLEAF), f32),
            VMEM((2 * WIN + 1, TLEAF, KF), bf16),
            VMEM((2 * WIN + 1, TLEAF, Q), f32),
        ] + pair_scratch(),
        compiler_params=params(40),
        cost_estimate=cost(9e9, 3e6),
        name="halo_terms",
    )(meta, lists_l, lists_r, pts_l, pts_r, v_all, f_all)
    got_r = lax.ppermute(halo_l, "tgt", backward)
    got_l = lax.ppermute(halo_r, "tgt", forward)

    bundle = jnp.concatenate(node_z + [top_sum], axis=0)
    ys = [bundle] + [lax.ppermute(bundle, "tgt", yshift[d]) for d in (1, 2, 3)]
    top_y = jnp.concatenate([y[4 * 288 :] for y in ys], axis=0)
    tops = jnp.concatenate([top_y] + [lax.ppermute(top_y, "tgt", zshift[d]) for d in (1, 2, 3)], axis=0)

    own = pl.pallas_call(
        own_kernel,
        out_shape=jax.ShapeDtypeStruct((WIN, TLEAF, Q), f32),
        in_specs=[smem, smem] + whole(3),
        out_specs=pl.BlockSpec(memory_space=VMEM),
        scratch_shapes=[
            VMEM((KF, TL_J * TLEAF), f32),
            VMEM((WIN + 1, TLEAF, KF), bf16),
            VMEM((WIN + 1, TLEAF, Q), f32),
        ] + pair_scratch(),
        compiler_params=params(40),
        cost_estimate=cost(5e9, 3e6),
        name="own_terms",
    )(meta, lists, target_points, v_all, f_all)

    partial = pl.pallas_call(
        node_kernel,
        out_shape=jax.ShapeDtypeStruct((2, 4, 16, TL_J * TLEAF), bf16),
        in_specs=[smem, smem] + whole(4) + [pl.BlockSpec(memory_space=pl.ANY)] * 4,
        out_specs=pl.BlockSpec(memory_space=VMEM),
        scratch_shapes=[
            VMEM((KF, TL_J * TLEAF), f32),
            VMEM((TL_J + 1, TLEAF, KF), bf16),
            VMEM((TL_J + 1, TLEAF, Q), f32),
            VMEM((4, 4 * 288 + 64, Q), bf16),
            VMEM((16, KF, 256), bf16),
            VMEM((16, 256, Q), bf16),
        ] + pair_scratch() + [pltpu.SemaphoreType.DMA((4,))],
        compiler_params=params(40),
        cost_estimate=cost(4e9, 3e6),
        name="node_terms",
    )(meta, lists, target_points, own, got_l, got_r, *ys)

    top_term = pl.pallas_call(
        top_kernel,
        out_shape=jax.ShapeDtypeStruct((16, TL_J * TLEAF), f32),
        in_specs=[smem, smem] + whole(2),
        out_specs=pl.BlockSpec(memory_space=VMEM),
        scratch_shapes=[
            VMEM((KF, TL_J * TLEAF), f32),
            VMEM((TL_J + 1, TLEAF, KF), bf16),
            VMEM((TL_J + 1, TLEAF, 16), f32),
            VMEM((16, KF, 256), bf16),
            VMEM((16, 256, 16), bf16),
            VMEM((KF, 256), f32),
        ] + pair_scratch(),
        compiler_params=params(40),
        cost_estimate=cost(8e9, 3e6),
        name="top_terms",
    )(meta, lists, target_points, tops)

    pair = partial[0].astype(f32) + lax.ppermute(partial[1], "src", cores).astype(f32)
    total = pair[0] + top_term
    for d in (1, 2, 3):
        total = total + lax.ppermute(pair[d].astype(bf16), "src", xshift[d]).astype(f32)
    return total.T


def solution(mesh):
    both = ("src", "tgt")
    in_specs = (
        P(None, both), P(both, None), P(both, None), P(both, None), P(both, None, None), P(both, None),
        P(both, None, None), P("tgt", None), P("tgt", None, "src"), P(None, "tgt"), P("src", "tgt", None),
        P("src", "tgt"), P("src", "tgt", None), P("src", "tgt"), P("src", "tgt", None), P("src", "tgt"),
        P("tgt", None), P("tgt"),
    )
    return jax.shard_map(shards, mesh=mesh, in_specs=in_specs, out_specs=P("tgt", "src"), check_vma=False)
```

```python
import functools

import jax
import jax.numpy as jnp
from jax import lax
from jax.experimental import pallas as pl
from jax.experimental.pallas import tpu as pltpu
from jax.sharding import PartitionSpec as P

SL = 8
LEAF = 512
SKEL = 256
Q = 128
TLEAF = 256
TL_J = 16
WIN = 6
KF = 16
LN2 = 0.6931471805599453
SCALE = 2.0 / LN2
GROUP = 16
TAIL = 4
VMEM = pltpu.VMEM
SMEM = pltpu.SMEM
bf16 = jnp.bfloat16
f32 = jnp.float32
NEAR_AT, FAR_AT, NODE_AT = 0, 8, 20
NEAR_N, FAR_N, NODE_N = 24, 25, 26
LIST_ROWS = 32
POINT_ROWS = 96
TRASH = 16
BIG = 60
HALO_COST = 6e9
OWN_COST = 5e9
NODE_COST = 6e9
TOP_COST = 6e9


def split2(x):
    high = x.astype(bf16).astype(f32)
    return high, (x - high).astype(bf16).astype(f32)


def split3(x):
    high, rest = split2(x)
    return high, rest, (x - high - rest).astype(bf16).astype(f32)


def centred(x):
    return (x - 1.0) * SCALE


def features(coords, is_source):
    pieces = [split2(c) for c in coords]
    high = [p[0] for p in pieces]
    low = [p[1] for p in pieces]
    norm = sum((h + r) * (h + r) for h, r in pieces)
    norms = list(split3(norm))
    one = jnp.ones_like(norm)
    zero = jnp.zeros_like(norm)
    if is_source:
        high = [-2.0 * h for h in high]
        low = [-2.0 * r for r in low]
        return high + low + high + [one, one, one] + norms + [zero]
    return high + high + low + norms + [one, one, one] + [zero]


def matern(w):
    w = jnp.maximum(w, 1e-12)
    u = w * lax.rsqrt(w)
    return ((1.0 + LN2 * u) * jnp.exp2(-u)).astype(bf16)


def take(row, index):
    return jnp.take_along_axis(row, index, axis=1, mode="promise_in_bounds")


def pick(chunks, index):
    low = index & 127
    high = index >> 7
    result = jnp.zeros((8, 128), f32)
    for k, chunk in enumerate(chunks):
        result = jnp.where(high == k, take(chunk, low), result)
    return result


def lanes(x, m):
    return x[:, 128 * m : 128 * (m + 1)]


def leaf_kernel(
    meta, idx_s, idx_h, piv_h, npiv_h, tpiv_h, pts_h, vals_h, proj_h, nproj_h, tproj_h,
    v_out, f_out, n_out, t_out, idx, piv, npiv, tpiv, pts, vals, proj, nproj, tproj,
    wide, gathered, fs, ns, sems,
):
    src, chip, core = meta[0], meta[1], meta[2]
    rows = vals.shape[0]
    moves = [(vals_h, vals), (proj_h, proj), (nproj_h, nproj), (tproj_h, tproj), (pts_h, pts), (idx_h, idx),
             (piv_h, piv), (npiv_h, npiv), (tpiv_h, tpiv)]
    copies = [pltpu.make_async_copy(a, b, sems.at[k]) for k, (a, b) in enumerate(moves)]
    for copy in copies:
        copy.start()
    copies[0].wait()

    def widen(k, _):
        at = pl.multiple_of(k * 512, 512)
        wide[pl.ds(at, 512), :] = vals[pl.ds(at, 512), :].astype(f32)
        return 0

    lax.fori_loop(0, rows // 512, widen, 0)

    def gather(k, _):
        at = pl.multiple_of(k * 64, 64)
        for r in range(64):
            gathered[pl.ds(at + r, 1), :] = wide[pl.ds(idx_s[at + r], 1), :]
        return 0

    lax.fori_loop(0, rows // 64, gather, 0)
    for copy in copies[1:]:
        copy.wait()

    for leaf in range(SL):
        leaf_vals = gathered[leaf * LEAF : (leaf + 1) * LEAF, :].astype(bf16)
        v_out[2 * leaf] = leaf_vals[:256]
        v_out[2 * leaf + 1] = leaf_vals[256:]
        v_out[16 + leaf] = jnp.dot(proj[leaf], leaf_vals, preferred_element_type=f32).astype(bf16)
    node_vals = jnp.dot(
        nproj[0], v_out[16:24].reshape(SL * SKEL, Q), preferred_element_type=f32
    ).astype(bf16)
    n_out[0:256, :] = node_vals
    top = jnp.dot(tproj[0], node_vals, preferred_element_type=f32).T

    index = idx[...]
    pivots = piv[...]
    node_piv = jnp.broadcast_to(npiv[...], (8, SKEL))
    top_piv = jnp.broadcast_to(tpiv[...], (8, SKEL))
    leaf_of = lax.broadcasted_iota(jnp.int32, (8, 128), 0)
    leaf_c, skel_c, node_c, top_c = [], [], [], []
    for c in range(3):
        chunks = [jnp.broadcast_to(pts[c : c + 1, 128 * k : 128 * (k + 1)], (8, 128)) for k in range(rows // 128)]
        leaf_x = [pick(chunks, lanes(index, m)) for m in range(4)]
        skel_x = [pick(leaf_x, lanes(pivots, m)) for m in range(2)]
        node_x = []
        top_x = []
        for m in range(2):
            at = lanes(node_piv, m)
            mine = jnp.where(leaf_of == (at >> 8), pick(skel_x, at & 255), 0.0)
            node_x.append(jnp.broadcast_to(jnp.sum(mine, axis=0, keepdims=True), (8, 128)))
        for m in range(2):
            at = lanes(top_piv, m)
            top_x.append(jnp.where((at >> 8) == src, centred(pick(node_x, at & 255)), 0.0))
        leaf_c.append(centred(jnp.concatenate(leaf_x, axis=1)))
        skel_c.append(centred(jnp.concatenate(skel_x, axis=1)))
        node_c.append(centred(jnp.concatenate(node_x, axis=1)))
        top_c.append(jnp.concatenate(top_x, axis=1))
    for f, (a, b, n) in enumerate(zip(features(leaf_c, True), features(skel_c, True), features(node_c, True))):
        for leaf in range(SL):
            fs[2 * leaf, f : f + 1, :] = a[leaf : leaf + 1, :256]
            fs[2 * leaf + 1, f : f + 1, :] = a[leaf : leaf + 1, 256:]
            fs[16 + leaf, f : f + 1, :] = b[leaf : leaf + 1, :]
        ns[f : f + 1, :] = n[0:1, :]
    f_out[...] = fs[...].astype(bf16)
    n_out[256:272, :] = ns[:, :128].astype(bf16)
    n_out[272:288, :] = ns[:, 128:].astype(bf16)
    ns[...] = jnp.zeros_like(ns)
    for c in range(3):
        for k, piece in enumerate(split3(top_c[c])):
            ns[3 * c + k : 3 * c + k + 1, :] = piece[0:1, :]
    pieces = ns[...].astype(bf16)
    for half in range(2):
        for x in range(4):
            for k in range(2):
                part = top[16 * (2 * x + k) : 16 * (2 * x + k) + 16, 128 * half : 128 * half + 128]
                at = (k ^ core, (x - chip) & 3)
                t_out[at[0], at[1], 32 * half : 32 * half + 16, :] = part.astype(bf16)
                t_out[at[0], at[1], 32 * half + 16 : 32 * half + 32, :] = lanes(pieces, half)


def target_rows(held, first, count, fa):
    step = TL_J * TLEAF // 128
    rows = features([centred(held[pl.ds(step * c + first, count), :]) for c in range(3)], False)
    for f, row in enumerate(rows):
        for k in range(count):
            fa[f : f + 1, 128 * k : 128 * k + 128] = row[k : k + 1, :]


def set_targets(fa, a_ref, count):
    for t in range(count):
        a_ref[t] = fa[:, TLEAF * t : TLEAF * t + TLEAF].T.astype(bf16)
    a_ref[count] = jnp.zeros((TLEAF, KF), bf16)


def run_pairs(pairs, n, trash, a_ref, f_ref, v_of, acc):
    for r in range(TAIL - 1):
        pairs[n + r] = trash

    def group(first, size):
        for q in range(size):
            pair = pairs[first + q]
            s = pair >> 5
            t = pair & 31
            w = jnp.dot(a_ref[t], f_ref[s], preferred_element_type=f32)
            acc[t] += jnp.dot(matern(w), v_of(s), preferred_element_type=f32)

    def large(g, _):
        group(g * GROUP, GROUP)
        return 0

    def small(g, _):
        group(done + g * TAIL, TAIL)
        return 0

    turns = n // GROUP
    done = turns * GROUP
    lax.fori_loop(0, turns, large, 0)
    lax.fori_loop(0, (n - done + TAIL - 1) // TAIL, small, 0)


def leaf_pairs(pairs, lists, start, base):
    def target(t, n):
        leaf = start + t

        def near(e, n):
            v = lists[NEAR_AT + e, leaf] - base
            pairs[n] = 64 * v + t
            pairs[n + 1] = 64 * v + 32 + t
            return n + jnp.where((v >= 0) & (v < SL), 2, 0)

        def far(e, n):
            v = lists[FAR_AT + e, leaf] - base
            pairs[n] = 512 + 32 * v + t
            return n + jnp.where((v >= 0) & (v < SL), 1, 0)

        n = lax.fori_loop(0, lists[NEAR_N, leaf], near, n)
        return lax.fori_loop(0, lists[FAR_N, leaf], far, n)

    return lax.fori_loop(0, WIN, target, 0)


def clear(acc):
    def one(t, _):
        acc[t] = jnp.zeros(acc.shape[1:], f32)
        return 0

    lax.fori_loop(0, acc.shape[0], one, 0)


def halo_kernel(base, meta, lists, held, v_ref, f_ref, after, out, fa, a_ref, acc, pairs):
    start = meta[6]
    clear(acc)
    target_rows(held, 2 * start, 2 * WIN, fa)
    set_targets(fa, a_ref, WIN)
    n = leaf_pairs(pairs, lists, start, base)
    run_pairs(pairs, n, WIN, a_ref, f_ref, lambda s: v_ref[s], acc)
    for t in range(WIN):
        out[t * TLEAF : (t + 1) * TLEAF, :] = acc[t].astype(bf16)


def own_kernel(meta, lists, held, v_ref, f_ref, after, out, a_all, fa, a_ref, pairs):
    start = meta[6]
    clear(out)
    target_rows(held, 0, 2 * TL_J, fa)
    set_targets(fa, a_all, TL_J)
    for t in range(WIN):
        a_ref[t] = a_all[start + t]
    a_ref[WIN] = jnp.zeros((TLEAF, KF), bf16)
    n = leaf_pairs(pairs, lists, start, SL)
    run_pairs(pairs, n, WIN, a_ref, f_ref, lambda s: v_ref[s], out)


def slot_of(column, row, plane):
    return 4 * ((row - (column >> 2)) & 3) + ((plane - (column & 3)) & 3)


def node_kernel(
    meta, lists, own, a_ref, halo_l, halo_r, y0, y1, y2, y3,
    out, acc, ys, f_ref, pairs, sems,
):
    core, chip, row, plane, start = meta[2], meta[1], meta[4], meta[5], meta[6]
    copies = [pltpu.make_async_copy(y, ys.at[k], sems.at[k]) for k, y in enumerate((y0, y1, y2, y3))]
    for copy in copies:
        copy.start()
    clear(acc)
    for t in range(WIN):
        sides = halo_l[t * TLEAF : (t + 1) * TLEAF, :].astype(f32) + halo_r[t * TLEAF : (t + 1) * TLEAF, :].astype(f32)
        acc[start + t] = own[t] + sides

    def target(t, n):
        def one(e, n):
            pairs[n] = 32 * slot_of(lists[NODE_AT + e, t], row, plane) + t
            return n + 1

        return lax.fori_loop(0, lists[NODE_N, t], one, n)

    n = lax.fori_loop(0, TL_J, target, 0)
    for copy in copies:
        copy.wait()
    for k in range(4):
        for z in range(4):
            f_ref[4 * k + z, :, 0:128] = ys[k, z * 288 + 256 : z * 288 + 272, :]
            f_ref[4 * k + z, :, 128:256] = ys[k, z * 288 + 272 : z * 288 + 288, :]

    def node_vals(s):
        return ys[s >> 2, pl.ds(pl.multiple_of((s & 3) * 288, 32), SKEL), :]

    run_pairs(pairs, n, TRASH, a_ref, f_ref, node_vals, acc)

    def turn(t, _):
        at = pl.multiple_of(t * TLEAF, TLEAF)
        block = acc[t].T
        for x in range(4):
            for k in range(2):
                begin = 16 * (2 * x + k)
                out[k ^ core, (x - chip) & 3, :, pl.ds(at, TLEAF)] = block[begin : begin + 16]
        return 0

    lax.fori_loop(0, TL_J, turn, 0)


def top_pairs(pairs, listed, counts, row, plane, first, count):
    def target(t, n):
        def one(e, n):
            pairs[n] = 32 * slot_of(listed[first + t, e], row, plane) + t
            return n + 1

        return lax.fori_loop(0, counts[first + t], one, n)

    return lax.fori_loop(0, count, target, 0)


def top_run(first, meta, listed, counts, a_all, f_ref, v_ref, out, a_ref, acc, pairs):
    count = TL_J // 2
    for t in range(count):
        a_ref[t] = a_all[first + t]
    a_ref[count] = jnp.zeros((TLEAF, KF), bf16)
    clear(acc)
    n = top_pairs(pairs, listed, counts, meta[4], meta[5], first, count)
    run_pairs(pairs, n, count, a_ref, f_ref, lambda s: v_ref[s], acc)
    for t in range(count):
        out[:, t * TLEAF : (t + 1) * TLEAF] = acc[t].T


def top_first(meta, listed, counts, a_all, tops, out, f_ref, v_ref, a_ref, acc, fw, pairs):
    for dz in range(4):
        for dy in range(4):
            slot = 4 * dy + dz
            base = (dz * 4 + dy) * 64
            for half in range(2):
                at = base + 32 * half
                vals = tops[at : at + 16, :].astype(f32)
                v_ref[slot, 128 * half : 128 * half + 128, :] = vals.T.astype(bf16)
                pieces = tops[at + 16 : at + 32, :].astype(f32)
                coords = [
                    pieces[3 * c : 3 * c + 1] + pieces[3 * c + 1 : 3 * c + 2] + pieces[3 * c + 2 : 3 * c + 3]
                    for c in range(3)
                ]
                for f, line in enumerate(features(coords, True)):
                    fw[f : f + 1, 128 * half : 128 * half + 128] = line
            f_ref[slot] = fw[...].astype(bf16)
    top_run(0, meta, listed, counts, a_all, f_ref, v_ref, out, a_ref, acc, pairs)


def top_second(meta, listed, counts, a_all, f_ref, v_ref, after, out, a_ref, acc, pairs):
    top_run(TL_J // 2, meta, listed, counts, a_all, f_ref, v_ref, out, a_ref, acc, pairs)


def whole(count):
    return [pl.BlockSpec(memory_space=VMEM)] * count


def params(mebibytes):
    return pltpu.CompilerParams(vmem_limit_bytes=mebibytes << 20)


def cost(flops, moved):
    return pl.CostEstimate(flops=int(flops), bytes_accessed=int(moved), transcendentals=0)


def pair_scratch():
    return [pltpu.SMEM((512,), jnp.int32)]


def shift(axis, count, fn):
    return [(i, fn(i)) for i in range(count) if 0 <= fn(i) < count]


def shards(
    source_points, source_values, leaf_index, leaf_pivots, leaf_proj, node_pivots, node_proj,
    top_pivots, top_proj, target_points, near_list, near_count, far_list, far_count,
    node_list, node_count, top_list, top_count,
):
    src = lax.axis_index("src")
    tgt = lax.axis_index("tgt")
    start = jnp.clip(2 * src - 2, 0, TL_J - WIN)
    meta = jnp.stack([src, src // 2, src % 2, tgt, tgt // 4, tgt % 4, start, src * 0]).astype(jnp.int32)
    lists = jnp.concatenate(
        [near_list[0].T, far_list[0].T, node_list[0].T, near_count, far_count, node_count,
         jnp.zeros((LIST_ROWS - 27, TL_J), jnp.int32)], axis=0)
    held = jnp.concatenate(
        [target_points.reshape(POINT_ROWS, 128), jnp.pad(lists.astype(f32), ((0, 0), (0, 128 - TL_J)))], axis=0)
    forward = shift("tgt", 16, lambda i: i + 1)
    backward = shift("tgt", 16, lambda i: i - 1)
    held_l = lax.ppermute(held, "tgt", forward)
    held_r = lax.ppermute(held, "tgt", backward)
    lists_l = held_l[POINT_ROWS:, :TL_J].astype(jnp.int32)
    lists_r = held_r[POINT_ROWS:, :TL_J].astype(jnp.int32)

    smem = pl.BlockSpec(memory_space=SMEM)
    anywhere = pl.BlockSpec(memory_space=pl.ANY)
    v_all, f_all, node_own, top_own = pl.pallas_call(
        leaf_kernel,
        out_shape=(
            jax.ShapeDtypeStruct((24, 256, Q), bf16),
            jax.ShapeDtypeStruct((24, KF, 256), bf16),
            jax.ShapeDtypeStruct((288, Q), bf16),
            jax.ShapeDtypeStruct((2, 4, 64, 128), bf16),
        ),
        in_specs=[smem, smem] + [anywhere] * 9,
        out_specs=tuple(whole(4)),
        scratch_shapes=[
            VMEM((8, 512), jnp.int32),
            VMEM((8, 256), jnp.int32),
            VMEM((1, 256), jnp.int32),
            VMEM((1, 256), jnp.int32),
            VMEM((3, 4096), f32),
            VMEM((4096, Q), bf16),
            VMEM((8, 256, 512), bf16),
            VMEM((1, 256, 2048), bf16),
            VMEM((1, 256, 256), bf16),
            VMEM((4096, Q), f32),
            VMEM((4096, Q), f32),
            VMEM((24, KF, 256), f32),
            VMEM((KF, 256), f32),
            pltpu.SemaphoreType.DMA((9,)),
        ],
        compiler_params=params(BIG),
        cost_estimate=cost(8e9, 8e6),
        name="leaf_stage",
    )(meta, leaf_index.reshape(-1), leaf_index, leaf_pivots, node_pivots, top_pivots, source_points, source_values,
      leaf_proj, node_proj, top_proj)

    zshift = [shift("tgt", 16, lambda i, d=d: (i // 4) * 4 + (i % 4 + d) % 4) for d in range(4)]
    yshift = [shift("tgt", 16, lambda i, d=d: ((i // 4 + d) % 4) * 4 + i % 4) for d in range(4)]
    xshift = [shift("src", 8, lambda i, d=d: (i + 2 * d) % 8) for d in range(4)]
    cores = shift("src", 8, lambda i: i ^ 1)

    def others(x, axis, shifts):
        return [lax.ppermute(x, axis, shifts[d]) for d in (1, 3, 2)]

    def in_order(x, got):
        return [x, got[0], got[2], got[1]]

    node_z = in_order(node_own, others(node_own, "tgt", zshift))
    top_pair = top_own[0].astype(f32) + lax.ppermute(top_own[1], "src", cores).astype(f32)
    bundle = jnp.concatenate(node_z, axis=0)
    ys = in_order(bundle, others(bundle, "tgt", yshift))
    top_sum = top_pair[0]
    for d in (1, 2, 3):
        top_sum = top_sum + lax.ppermute(top_pair[d].astype(bf16), "src", xshift[d]).astype(f32)
    top_sum = top_sum.astype(bf16)

    def halo(base, lists_of, held_of, after):
        return pl.pallas_call(
            functools.partial(halo_kernel, base),
            out_shape=jax.ShapeDtypeStruct((WIN * TLEAF, Q), bf16),
            in_specs=[smem, smem] + whole(3) + [anywhere],
            out_specs=pl.BlockSpec(memory_space=VMEM),
            scratch_shapes=[
                VMEM((KF, WIN * TLEAF), f32),
                VMEM((WIN + 1, TLEAF, KF), bf16),
                VMEM((WIN + 1, TLEAF, Q), f32),
            ] + pair_scratch(),
            compiler_params=params(40),
            cost_estimate=cost(HALO_COST, 3e6),
            name="halo_terms",
        )(meta, lists_of, held_of, v_all, f_all, after)

    to_l = halo(16, lists_l, held_l, v_all)
    got_r = lax.ppermute(to_l, "tgt", backward)
    to_r = halo(0, lists_r, held_r, bundle)
    got_l = lax.ppermute(to_r, "tgt", forward)

    top_y = jnp.concatenate(in_order(top_sum, others(top_sum, "tgt", yshift)), axis=0)
    tops = jnp.concatenate(in_order(top_y, others(top_y, "tgt", zshift)), axis=0)

    own, a_all = pl.pallas_call(
        own_kernel,
        out_shape=(
            jax.ShapeDtypeStruct((WIN + 1, TLEAF, Q), f32),
            jax.ShapeDtypeStruct((TL_J + 1, TLEAF, KF), bf16),
        ),
        in_specs=[smem, smem] + whole(3) + [anywhere],
        out_specs=tuple(whole(2)),
        scratch_shapes=[
            VMEM((KF, TL_J * TLEAF), f32),
            VMEM((WIN + 1, TLEAF, KF), bf16),
        ] + pair_scratch(),
        compiler_params=params(40),
        cost_estimate=cost(OWN_COST, 3e6),
        name="own_terms",
    )(meta, lists, held, v_all, f_all, to_r)

    partial = pl.pallas_call(
        node_kernel,
        out_shape=jax.ShapeDtypeStruct((2, 4, 16, TL_J * TLEAF), f32),
        in_specs=[smem, smem] + whole(4) + [anywhere] * 4,
        out_specs=pl.BlockSpec(memory_space=VMEM),
        scratch_shapes=[
            VMEM((TL_J + 1, TLEAF, Q), f32),
            VMEM((4, 4 * 288, Q), bf16),
            VMEM((16, KF, 256), bf16),
        ] + pair_scratch() + [pltpu.SemaphoreType.DMA((4,))],
        compiler_params=params(40),
        cost_estimate=cost(NODE_COST, 3e6),
        name="node_terms",
    )(meta, lists, own, a_all, got_l, got_r, *ys)

    half = TL_J // 2
    top_scratch = [VMEM((half + 1, TLEAF, KF), bf16), VMEM((half + 1, TLEAF, 16), f32)]
    half_out = jax.ShapeDtypeStruct((16, half * TLEAF), f32)
    low, top_f, top_v = pl.pallas_call(
        top_first,
        out_shape=(
            half_out,
            jax.ShapeDtypeStruct((16, KF, 256), bf16),
            jax.ShapeDtypeStruct((16, 256, 16), bf16),
        ),
        in_specs=[smem, smem, smem] + whole(2),
        out_specs=tuple(whole(3)),
        scratch_shapes=top_scratch + [VMEM((KF, 256), f32)] + pair_scratch(),
        compiler_params=params(40),
        cost_estimate=cost(TOP_COST, 3e6),
        name="top_first",
    )(meta, top_list, top_count, a_all, tops)

    pair = partial[0] + lax.ppermute(partial[1], "src", cores)
    high = pl.pallas_call(
        top_second,
        out_shape=half_out,
        in_specs=[smem, smem, smem] + whole(3) + [anywhere],
        out_specs=pl.BlockSpec(memory_space=VMEM),
        scratch_shapes=top_scratch + pair_scratch(),
        compiler_params=params(40),
        cost_estimate=cost(TOP_COST, 3e6),
        name="top_second",
    )(meta, top_list, top_count, a_all, top_f, top_v, pair)

    total = pair[0] + jnp.concatenate([low, high], axis=1)
    for d in (1, 3, 2):
        total = total + lax.ppermute(pair[d].astype(bf16), "src", xshift[d]).astype(f32)
    return total.T


def solution(mesh):
    both = ("src", "tgt")
    in_specs = (
        P(None, both), P(both, None), P(both, None), P(both, None), P(both, None, None), P(both, None),
        P(both, None, None), P("tgt", None), P("tgt", None, "src"), P(None, "tgt"), P("src", "tgt", None),
        P("src", "tgt"), P("src", "tgt", None), P("src", "tgt"), P("src", "tgt", None), P("src", "tgt"),
        P("tgt", None), P("tgt"),
    )
    return jax.shard_map(shards, mesh=mesh, in_specs=in_specs, out_specs=P("tgt", "src"), check_vma=False)
```

```python
import functools

import jax
import jax.numpy as jnp
from jax import lax
from jax.experimental import pallas as pl
from jax.experimental.pallas import tpu as pltpu
from jax.sharding import PartitionSpec as P

SL = 8
LEAF = 512
SKEL = 256
Q = 128
TLEAF = 256
TL_J = 16
WIN = 6
KF = 16
LN2 = 0.6931471805599453
SCALE = 2.0 / LN2
GROUP = 16
TAIL = 4
VMEM = pltpu.VMEM
SMEM = pltpu.SMEM
bf16 = jnp.bfloat16
f32 = jnp.float32
NEAR_AT, FAR_AT, NODE_AT = 0, 8, 20
NEAR_N, FAR_N, NODE_N = 24, 25, 26
LIST_ROWS = 32
POINT_ROWS = 96
TRASH = 16
PART = 384
BIG = 60
OUT = pltpu.VMEM
HALO_COST = 6e9
OWN_COST = 5e9
NODE_COST = 6e9
TOP_COST = 6e9


def split2(x):
    high = x.astype(bf16).astype(f32)
    return high, (x - high).astype(bf16).astype(f32)


def split3(x):
    high, rest = split2(x)
    return high, rest, (x - high - rest).astype(bf16).astype(f32)


def centred(x):
    return (x - 1.0) * SCALE


def features(coords, is_source):
    pieces = [split2(c) for c in coords]
    high = [p[0] for p in pieces]
    low = [p[1] for p in pieces]
    norm = sum((h + r) * (h + r) for h, r in pieces)
    norms = list(split3(norm))
    one = jnp.ones_like(norm)
    zero = jnp.zeros_like(norm)
    if is_source:
        high = [-2.0 * h for h in high]
        low = [-2.0 * r for r in low]
        return high + low + high + [one, one, one] + norms + [zero]
    return high + high + low + norms + [one, one, one] + [zero]


def matern(w):
    w = jnp.maximum(w, 1e-12)
    u = w * lax.rsqrt(w)
    return ((1.0 + LN2 * u) * jnp.exp2(-u)).astype(bf16)


def take(row, index):
    return jnp.take_along_axis(row, index, axis=1, mode="promise_in_bounds")


def pick(chunks, index):
    low = index & 127
    high = index >> 7
    result = jnp.zeros((8, 128), f32)
    for k, chunk in enumerate(chunks):
        result = jnp.where(high == k, take(chunk, low), result)
    return result


def lanes(x, m):
    return x[:, 128 * m : 128 * (m + 1)]


def place():
    src = lax.axis_index("src")
    tgt = lax.axis_index("tgt")
    start = jnp.clip(2 * src - 2, 0, TL_J - WIN)
    return src, src >> 1, src & 1, tgt >> 2, tgt & 3, start


def leaf_kernel(
    idx_h, piv_h, npiv_h, tpiv_h, pts_h, vals_h, proj_h, nproj_h, tproj_h,
    tpts_h, near_h, far_h, node_h, nearn_h, farn_h, noden_h,
    v_out, f_out, n_out, t_out, held_out, lists_out, idx, piv, npiv, tpiv, pts, vals, proj, nproj, tproj,
    tpts, near, far, node, nearn, farn, noden, wide, gathered, fs, ns, idx_s, sems,
):
    src, chip, _, _, _, _ = place()
    rows = vals.shape[0]
    moves = [(pts_h, pts), (idx_h, idx), (piv_h, piv), (npiv_h, npiv), (tpiv_h, tpiv), (vals_h, vals),
             (proj_h, proj), (nproj_h, nproj), (tproj_h, tproj), (tpts_h, tpts), (near_h, near), (far_h, far),
             (node_h, node), (nearn_h, nearn), (farn_h, farn), (noden_h, noden)]
    copies = [pltpu.make_async_copy(a, b, sems.at[k]) for k, (a, b) in enumerate(moves)]
    for leaf in range(SL):
        copies.append(pltpu.make_async_copy(idx_h.at[leaf], idx_s.at[pl.ds(LEAF * leaf, LEAF)], sems.at[16 + leaf]))
    for copy in copies:
        copy.start()
    for copy in copies[:5]:
        copy.wait()
    index = idx[...]
    pivots = piv[...]
    node_piv = jnp.broadcast_to(npiv[...], (8, SKEL))
    top_piv = jnp.broadcast_to(tpiv[...], (8, SKEL))
    leaf_of = lax.broadcasted_iota(jnp.int32, (8, 128), 0)
    leaf_c, skel_c, node_c, top_c = [], [], [], []
    for c in range(3):
        chunks = [jnp.broadcast_to(pts[c : c + 1, 128 * k : 128 * (k + 1)], (8, 128)) for k in range(rows // 128)]
        leaf_x = [pick(chunks, lanes(index, m)) for m in range(4)]
        skel_x = [pick(leaf_x, lanes(pivots, m)) for m in range(2)]
        node_x = []
        top_x = []
        for m in range(2):
            at = lanes(node_piv, m)
            mine = jnp.where(leaf_of == (at >> 8), pick(skel_x, at & 255), 0.0)
            node_x.append(jnp.broadcast_to(jnp.sum(mine, axis=0, keepdims=True), (8, 128)))
        for m in range(2):
            at = lanes(top_piv, m)
            top_x.append(jnp.where((at >> 8) == src, centred(pick(node_x, at & 255)), 0.0))
        leaf_c.append(centred(jnp.concatenate(leaf_x, axis=1)))
        skel_c.append(centred(jnp.concatenate(skel_x, axis=1)))
        node_c.append(centred(jnp.concatenate(node_x, axis=1)))
        top_c.append(jnp.concatenate(top_x, axis=1))
    for f, (a, b, n) in enumerate(zip(features(leaf_c, True), features(skel_c, True), features(node_c, True))):
        for leaf in range(SL):
            fs[2 * leaf, f : f + 1, :] = a[leaf : leaf + 1, :256]
            fs[2 * leaf + 1, f : f + 1, :] = a[leaf : leaf + 1, 256:]
            fs[16 + leaf, f : f + 1, :] = b[leaf : leaf + 1, :]
        ns[f : f + 1, :] = n[0:1, :]
    f_out[...] = fs[...].astype(bf16)
    n_out[256:272, :] = ns[:, :128].astype(bf16)
    n_out[272:288, :] = ns[:, 128:].astype(bf16)
    ns[...] = jnp.zeros_like(ns)
    for c in range(3):
        for k, piece in enumerate(split3(top_c[c])):
            ns[3 * c + k : 3 * c + k + 1, :] = piece[0:1, :]
    pieces = ns[...].astype(bf16)
    for copy in copies[9:]:
        copy.wait()
    step = POINT_ROWS // 3
    for c in range(3):
        for k in range(step):
            held_out[step * c + k : step * c + k + 1, :] = tpts[c : c + 1, 128 * k : 128 * k + 128]
    lists_out[...] = jnp.zeros_like(lists_out)
    lists_out[NEAR_AT : FAR_AT, :] = near[0]
    for e in range(NODE_AT - FAR_AT):
        lists_out[FAR_AT + e : FAR_AT + e + 1, :] = far[e]
    lists_out[NODE_AT : NEAR_N, :] = node[0]
    lists_out[NEAR_N : NEAR_N + 1, :] = nearn[...]
    lists_out[FAR_N : FAR_N + 1, :] = farn[...]
    lists_out[NODE_N : NODE_N + 1, :] = noden[...]
    held_out[POINT_ROWS:, :] = jnp.zeros((LIST_ROWS, 128), f32)
    held_out[POINT_ROWS:, :TL_J] = lists_out[...].astype(f32)
    copies[5].wait()

    def widen(k, _):
        at = pl.multiple_of(k * 512, 512)
        wide[pl.ds(at, 512), :] = vals[pl.ds(at, 512), :].astype(f32)
        return 0

    lax.fori_loop(0, rows // 512, widen, 0)

    def gather(k, _):
        at = pl.multiple_of(k * 64, 64)
        for r in range(64):
            gathered[pl.ds(at + r, 1), :] = wide[pl.ds(idx_s[at + r], 1), :]
        return 0

    lax.fori_loop(0, rows // 64, gather, 0)
    for copy in copies[6:9]:
        copy.wait()

    for leaf in range(SL):
        leaf_vals = gathered[leaf * LEAF : (leaf + 1) * LEAF, :].astype(bf16)
        v_out[2 * leaf] = leaf_vals[:256]
        v_out[2 * leaf + 1] = leaf_vals[256:]
        v_out[16 + leaf] = jnp.dot(proj[leaf], leaf_vals, preferred_element_type=f32).astype(bf16)
    node_vals = jnp.dot(
        nproj[0], v_out[16:24].reshape(SL * SKEL, Q), preferred_element_type=f32
    ).astype(bf16)
    n_out[0:256, :] = node_vals
    top = jnp.dot(tproj[0], node_vals, preferred_element_type=f32).T

    for half in range(2):
        for x in range(4):
            part = top[32 * x : 32 * x + 32, 128 * half : 128 * half + 128]
            at = (x - chip) & 3
            t_out[at, 48 * half : 48 * half + 32, :] = part.astype(bf16)
            t_out[at, 48 * half + 32 : 48 * half + 48, :] = lanes(pieces, half)


def target_rows(held, first, count, fa):
    step = TL_J * TLEAF // 128
    rows = features([centred(held[pl.ds(step * c + first, count), :]) for c in range(3)], False)
    for f, row in enumerate(rows):
        for k in range(count):
            fa[f : f + 1, 128 * k : 128 * k + 128] = row[k : k + 1, :]


def set_targets(fa, a_ref, count):
    for t in range(count):
        a_ref[t] = fa[:, TLEAF * t : TLEAF * t + TLEAF].T.astype(bf16)
    a_ref[count] = jnp.zeros((TLEAF, KF), bf16)


def run_pairs(pairs, n, trash, a_ref, f_ref, v_of, acc):
    for r in range(TAIL - 1):
        pairs[n + r] = trash

    def group(first, size):
        for q in range(size):
            pair = pairs[first + q]
            s = pair >> 5
            t = pair & 31
            w = jnp.dot(a_ref[t], f_ref[s], preferred_element_type=f32)
            acc[t] += jnp.dot(matern(w), v_of(s), preferred_element_type=f32)

    def large(g, _):
        group(g * GROUP, GROUP)
        return 0

    def small(g, _):
        group(done + g * TAIL, TAIL)
        return 0

    turns = n // GROUP
    done = turns * GROUP
    lax.fori_loop(0, turns, large, 0)
    lax.fori_loop(0, (n - done + TAIL - 1) // TAIL, small, 0)


def leaf_pairs(pairs, lists, start, base):
    def target(t, n):
        leaf = start + t
        near, far = lists[NEAR_N, leaf], lists[FAR_N, leaf]
        for e in range(FAR_AT):
            v = lists[NEAR_AT + e, leaf] - base
            pairs[n] = 64 * v + t
            pairs[n + 1] = 64 * v + 32 + t
            n = n + jnp.where((v >= 0) & (v < SL) & (e < near), 2, 0)
        for e in range(NODE_AT - FAR_AT):
            v = lists[FAR_AT + e, leaf] - base
            pairs[n] = 512 + 32 * v + t
            n = n + jnp.where((v >= 0) & (v < SL) & (e < far), 1, 0)
        return n

    return lax.fori_loop(0, WIN, target, 0)


def clear(acc):
    def one(t, _):
        acc[t] = jnp.zeros(acc.shape[1:], f32)
        return 0

    lax.fori_loop(0, acc.shape[0], one, 0)


def halo_kernel(base, lists, held, v_ref, f_ref, after, out, fa, a_ref, acc, pairs):
    start = place()[5]
    clear(acc)
    target_rows(held, 2 * start, 2 * WIN, fa)
    set_targets(fa, a_ref, WIN)
    n = leaf_pairs(pairs, lists, start, base)
    run_pairs(pairs, n, WIN, a_ref, f_ref, lambda s: v_ref[s], acc)
    for t in range(WIN):
        out[t * TLEAF : (t + 1) * TLEAF, :] = acc[t].astype(bf16)


def own_kernel(lists, held, v_ref, f_ref, after, out, a_all, fa, a_ref, pairs):
    start = place()[5]
    clear(out)
    target_rows(held, 0, 2 * TL_J, fa)
    set_targets(fa, a_all, TL_J)
    for t in range(WIN):
        a_ref[t] = a_all[start + t]
    a_ref[WIN] = jnp.zeros((TLEAF, KF), bf16)
    n = leaf_pairs(pairs, lists, start, SL)
    run_pairs(pairs, n, WIN, a_ref, f_ref, lambda s: v_ref[s], out)


def slot_of(column, row, plane):
    return 4 * ((row - (column >> 2)) & 3) + ((plane - (column & 3)) & 3)


def node_kernel(
    lists, own, a_ref, halo_l, halo_r, top, y0, y1, y2, y3,
    out, acc, ys, f_ref, pairs, sems,
):
    _, chip, core, row, plane, start = place()
    copies = [pltpu.make_async_copy(y, ys.at[k], sems.at[k]) for k, y in enumerate((y0, y1, y2, y3))]
    for copy in copies:
        copy.start()
    clear(acc)
    for t in range(WIN):
        sides = halo_l[t * TLEAF : (t + 1) * TLEAF, :].astype(f32) + halo_r[t * TLEAF : (t + 1) * TLEAF, :].astype(f32)
        acc[start + t] = own[t] + sides

    def target(t, n):
        for e in range(NEAR_N - NODE_AT):
            pairs[n + e] = 32 * slot_of(lists[NODE_AT + e, t], row, plane) + t
        return n + lists[NODE_N, t]

    n = lax.fori_loop(0, TL_J, target, 0)
    for copy in copies:
        copy.wait()
    for k in range(4):
        for z in range(4):
            f_ref[4 * k + z, :, 0:128] = ys[k, z * PART + 256 : z * PART + 272, :]
            f_ref[4 * k + z, :, 128:256] = ys[k, z * PART + 272 : z * PART + 288, :]

    def node_vals(s):
        return ys[s >> 2, pl.ds(pl.multiple_of((s & 3) * PART, 32), SKEL), :]

    run_pairs(pairs, n, TRASH, a_ref, f_ref, node_vals, acc)

    def turn(t, _):
        at = pl.multiple_of(t * TLEAF, TLEAF)
        block = acc[t].T
        for x in range(4):
            for k in range(2):
                begin = 16 * (2 * x + k)
                out[k ^ core, (x - chip) & 3, :, pl.ds(at, TLEAF)] = block[begin : begin + 16]
        return 0

    lax.fori_loop(0, TL_J, turn, 0)
    for t in range(TL_J // 2):
        at = pl.multiple_of((core * (TL_J // 2) + t) * TLEAF, TLEAF)
        for k in range(2):
            out[k, 0, :, pl.ds(at, TLEAF)] += top[k, :, t * TLEAF : (t + 1) * TLEAF]


def top_pairs(pairs, listed, counts, row, plane, first, count):
    def target(t, n):
        for e in range(listed.shape[1]):
            pairs[n + e] = 32 * slot_of(listed[first + t, e], row, plane) + t
        return n + counts[first + t]

    return lax.fori_loop(0, count, target, 0)


def top_kernel(listed, counts, a_all, y0, y1, y2, y3, out, f_ref, v_ref, a_ref, acc, pw, fw, pairs):
    count = TL_J // 2
    _, _, core, row, plane, _ = place()
    first = core * count
    for dy, ys in enumerate((y0, y1, y2, y3)):
        for dz in range(4):
            slot = 4 * dy + dz
            for half in range(2):
                at = dz * PART + 288 + 48 * half
                vals = ys[at : at + 32, :].astype(f32)
                v_ref[slot, 128 * half : 128 * half + 128, :] = vals.T.astype(bf16)
                pieces = ys[at + 32 : at + 48, :].astype(f32)
                line = 2 * slot + half
                for p in range(9):
                    pw[p, line : line + 1, :] = pieces[p : p + 1]
    coords = [pw[3 * c] + pw[3 * c + 1] + pw[3 * c + 2] for c in range(3)]
    for f, lines in enumerate(features(coords, True)):
        for line in range(32):
            half = line % 2
            fw[line // 2, f : f + 1, 128 * half : 128 * half + 128] = lines[line : line + 1, :]
    f_ref[...] = fw[...].astype(bf16)
    for t in range(count):
        a_ref[t] = a_all[first + t]
    a_ref[count] = jnp.zeros((TLEAF, KF), bf16)
    clear(acc)
    n = top_pairs(pairs, listed, counts, row, plane, first, count)
    run_pairs(pairs, n, count, a_ref, f_ref, lambda s: v_ref[s], acc)
    for t in range(count):
        block = acc[t].T
        for k in range(2):
            out[k ^ core, :, t * TLEAF : (t + 1) * TLEAF] = block[16 * k : 16 * k + 16]


def whole(count):
    return [pl.BlockSpec(memory_space=VMEM)] * count


def params(mebibytes):
    return pltpu.CompilerParams(vmem_limit_bytes=mebibytes << 20)


def cost(flops, moved):
    return pl.CostEstimate(flops=int(flops), bytes_accessed=int(moved), transcendentals=0)


def pair_scratch():
    return [pltpu.SMEM((512,), jnp.int32)]


def shift(axis, count, fn):
    return [(i, fn(i)) for i in range(count) if 0 <= fn(i) < count]


def shards(
    source_points, source_values, leaf_index, leaf_pivots, leaf_proj, node_pivots, node_proj,
    top_pivots, top_proj, target_points, near_list, near_count, far_list, far_count,
    node_list, node_count, top_list, top_count,
):
    smem = pl.BlockSpec(memory_space=SMEM)
    anywhere = pl.BlockSpec(memory_space=pl.ANY)
    v_all, f_all, node_own, top_own, held, lists = pl.pallas_call(
        leaf_kernel,
        out_shape=(
            OUT((24, 256, Q), bf16),
            OUT((24, KF, 256), bf16),
            OUT((288, Q), bf16),
            OUT((4, 96, 128), bf16),
            OUT((POINT_ROWS + LIST_ROWS, 128), f32),
            OUT((LIST_ROWS, TL_J), jnp.int32),
        ),
        in_specs=[anywhere] * 16,
        out_specs=tuple(whole(6)),
        scratch_shapes=[
            VMEM((8, 512), jnp.int32),
            VMEM((8, 256), jnp.int32),
            VMEM((1, 256), jnp.int32),
            VMEM((1, 256), jnp.int32),
            VMEM((3, 4096), f32),
            VMEM((4096, Q), bf16),
            VMEM((8, 256, 512), bf16),
            VMEM((1, 256, 2048), bf16),
            VMEM((1, 256, 256), bf16),
            VMEM((3, 4096), f32),
            VMEM((1, 8, TL_J), jnp.int32),
            VMEM((12, 1, TL_J), jnp.int32),
            VMEM((1, 4, TL_J), jnp.int32),
            VMEM((1, TL_J), jnp.int32),
            VMEM((1, TL_J), jnp.int32),
            VMEM((1, TL_J), jnp.int32),
            VMEM((4096, Q), f32),
            VMEM((4096, Q), f32),
            VMEM((24, KF, 256), f32),
            VMEM((KF, 256), f32),
            pltpu.SMEM((4096,), jnp.int32),
            pltpu.SemaphoreType.DMA((24,)),
        ],
        compiler_params=params(BIG),
        cost_estimate=cost(8e9, 8e6),
        name="leaf_stage",
    )(leaf_index, leaf_pivots, node_pivots, top_pivots, source_points, source_values,
      leaf_proj, node_proj, top_proj, target_points, near_list.transpose(0, 2, 1), far_list.transpose(2, 0, 1),
      node_list.transpose(0, 2, 1), near_count, far_count, node_count)
    forward = shift("tgt", 16, lambda i: i + 1)
    backward = shift("tgt", 16, lambda i: i - 1)
    held_l = lax.ppermute(held, "tgt", forward)
    held_r = lax.ppermute(held, "tgt", backward)
    lists_l = held_l[POINT_ROWS:, :TL_J].astype(jnp.int32)
    lists_r = held_r[POINT_ROWS:, :TL_J].astype(jnp.int32)

    zshift = [shift("tgt", 16, lambda i, d=d: (i // 4) * 4 + (i % 4 + d) % 4) for d in range(4)]
    yshift = [shift("tgt", 16, lambda i, d=d: ((i // 4 + d) % 4) * 4 + i % 4) for d in range(4)]
    xshift = [shift("src", 8, lambda i, d=d: (i + 2 * d) % 8) for d in range(4)]
    cores = shift("src", 8, lambda i: i ^ 1)

    def others(x, axis, shifts):
        return [lax.ppermute(x, axis, shifts[d]) for d in (1, 3, 2)]

    def in_order(x, got):
        return [x, got[0], got[2], got[1]]

    top_pair = top_own.astype(f32) + lax.ppermute(top_own, "src", cores).astype(f32)
    top_sum = top_pair[0]
    for d in (1, 3, 2):
        top_sum = top_sum + lax.ppermute(top_pair[d].astype(bf16), "src", xshift[d]).astype(f32)
    parts = jnp.concatenate([node_own, top_sum.astype(bf16)], axis=0)
    bundle = jnp.concatenate(in_order(parts, others(parts, "tgt", zshift)), axis=0)
    ys = in_order(bundle, others(bundle, "tgt", yshift))

    def halo(base, lists_of, held_of, after):
        return pl.pallas_call(
            functools.partial(halo_kernel, base),
            out_shape=jax.ShapeDtypeStruct((WIN * TLEAF, Q), bf16),
            in_specs=[smem] + whole(3) + [anywhere],
            out_specs=pl.BlockSpec(memory_space=VMEM),
            scratch_shapes=[
                VMEM((KF, WIN * TLEAF), f32),
                VMEM((WIN + 1, TLEAF, KF), bf16),
                VMEM((WIN + 1, TLEAF, Q), f32),
            ] + pair_scratch(),
            compiler_params=params(24),
            cost_estimate=cost(HALO_COST, 3e6),
            name="halo_terms",
        )(lists_of, held_of, v_all, f_all, after)

    to_l = halo(16, lists_l, held_l, parts)
    got_r = lax.ppermute(to_l, "tgt", backward)
    to_r = halo(0, lists_r, held_r, bundle)
    got_l = lax.ppermute(to_r, "tgt", forward)

    own, a_all = pl.pallas_call(
        own_kernel,
        out_shape=(
            jax.ShapeDtypeStruct((WIN + 1, TLEAF, Q), f32),
            jax.ShapeDtypeStruct((TL_J + 1, TLEAF, KF), bf16),
        ),
        in_specs=[smem] + whole(3) + [anywhere],
        out_specs=tuple(whole(2)),
        scratch_shapes=[
            VMEM((KF, TL_J * TLEAF), f32),
            VMEM((WIN + 1, TLEAF, KF), bf16),
        ] + pair_scratch(),
        compiler_params=params(24),
        cost_estimate=cost(OWN_COST, 3e6),
        name="own_terms",
    )(lists, held, v_all, f_all, to_r)

    half = TL_J // 2
    top_term = pl.pallas_call(
        top_kernel,
        out_shape=jax.ShapeDtypeStruct((2, 16, half * TLEAF), f32),
        in_specs=[smem, smem] + whole(5),
        out_specs=pl.BlockSpec(memory_space=VMEM),
        scratch_shapes=[
            VMEM((16, KF, 256), bf16),
            VMEM((16, 256, 32), bf16),
            VMEM((half + 1, TLEAF, KF), bf16),
            VMEM((half + 1, TLEAF, 32), f32),
            VMEM((9, 32, 128), f32),
            VMEM((16, KF, 256), f32),
        ] + pair_scratch(),
        compiler_params=params(24),
        cost_estimate=cost(TOP_COST, 3e6),
        name="top_terms",
    )(top_list, top_count, a_all, *ys)

    partial = pl.pallas_call(
        node_kernel,
        out_shape=jax.ShapeDtypeStruct((2, 4, 16, TL_J * TLEAF), f32),
        in_specs=[smem] + whole(5) + [anywhere] * 4,
        out_specs=pl.BlockSpec(memory_space=VMEM),
        scratch_shapes=[
            VMEM((TL_J + 1, TLEAF, Q), f32),
            VMEM((4, 4 * PART, Q), bf16),
            VMEM((16, KF, 256), bf16),
        ] + pair_scratch() + [pltpu.SemaphoreType.DMA((4,))],
        compiler_params=params(24),
        cost_estimate=cost(NODE_COST, 3e6),
        name="node_terms",
    )(lists, own, a_all, got_l, got_r, top_term, *ys)

    pair = partial[0] + lax.ppermute(partial[1], "src", cores)
    total = pair[0]
    for d in (1, 3, 2):
        total = total + lax.ppermute(pair[d].astype(bf16), "src", xshift[d]).astype(f32)
    return total.T


def solution(mesh):
    both = ("src", "tgt")
    in_specs = (
        P(None, both), P(both, None), P(both, None), P(both, None), P(both, None, None), P(both, None),
        P(both, None, None), P("tgt", None), P("tgt", None, "src"), P(None, "tgt"), P("src", "tgt", None),
        P("src", "tgt"), P("src", "tgt", None), P("src", "tgt"), P("src", "tgt", None), P("src", "tgt"),
        P("tgt", None), P("tgt"),
    )
    return jax.shard_map(shards, mesh=mesh, in_specs=in_specs, out_specs=P("tgt", "src"), check_vma=False)
```

```python
import functools

import jax
import jax.numpy as jnp
from jax import lax
from jax.experimental import pallas as pl
from jax.experimental.pallas import tpu as pltpu
from jax.sharding import PartitionSpec as P

SL = 8
LEAF = 512
SKEL = 256
Q = 128
TLEAF = 256
TL_J = 16
WIN = 6
KF = 16
LN2 = 0.6931471805599453
SCALE = 2.0
GROUP = 16
TAIL = 4
VMEM = pltpu.VMEM
SMEM = pltpu.SMEM
bf16 = jnp.bfloat16
f32 = jnp.float32
NEAR_AT, FAR_AT, NODE_AT = 0, 8, 20
NEAR_N, FAR_N, NODE_N = 24, 25, 26
LIST_ROWS = 32
POINT_ROWS = 96
HELD = 3 * POINT_ROWS + LIST_ROWS
TRASH = 16
PART = 384
BIG = 60
OUT = pltpu.VMEM
HALO_COST = 1e9
OWN_COST = 5e9
NODE_COST = 6e9
TOP_COST = 6e9


def split2(x):
    high = x.astype(bf16).astype(f32)
    return high, (x - high).astype(bf16).astype(f32)


def split3(x):
    high, rest = split2(x)
    return high, rest, (x - high - rest).astype(bf16).astype(f32)


def centred(x):
    return (x - 1.0) * SCALE


def features(coords, is_source):
    pieces = [split2(c) for c in coords]
    high = [p[0] for p in pieces]
    low = [p[1] for p in pieces]
    norm = sum((h + r) * (h + r) for h, r in pieces)
    norms = list(split3(norm))
    one = jnp.ones_like(norm)
    zero = jnp.zeros_like(norm)
    if is_source:
        high = [-2.0 * h for h in high]
        low = [-2.0 * r for r in low]
        return high + low + high + [one, one, one] + norms + [zero]
    return high + high + low + norms + [one, one, one] + [zero]


def matern(w):
    w = jnp.maximum(w, 1e-12)
    u = w * lax.rsqrt(w)
    return ((1.0 + u) * jnp.exp2(u * (-1.0 / LN2))).astype(bf16)


def take(row, index):
    return jnp.take_along_axis(row, index, axis=1, mode="promise_in_bounds")


def pick(chunks, index):
    low = index & 127
    high = index >> 7
    result = jnp.zeros((8, 128), f32)
    for k, chunk in enumerate(chunks):
        result = jnp.where(high == k, take(chunk, low), result)
    return result


def lanes(x, m):
    return x[:, 128 * m : 128 * (m + 1)]


def place():
    src = lax.axis_index("src")
    tgt = lax.axis_index("tgt")
    start = jnp.clip(2 * src - 2, 0, TL_J - WIN)
    return src, src >> 1, src & 1, tgt, start


def leaf_kernel(
    idx_h, piv_h, npiv_h, tpiv_h, pts_h, vals_h, proj_h, nproj_h, tproj_h,
    tpts_h, near_h, far_h, node_h, nearn_h, farn_h, noden_h,
    v_out, f_out, n_out, t_out, held_out, lists_out, idx, piv, npiv, tpiv, pts, vals, proj, nproj, tproj,
    tpts, near, far, node, nearn, farn, noden, wide, gathered, fs, ns, hf, lf, idx_s, sems,
):
    src, chip, _, _, _ = place()
    rows = vals.shape[0]
    moves = [(pts_h, pts), (idx_h, idx), (piv_h, piv), (npiv_h, npiv), (tpiv_h, tpiv), (vals_h, vals),
             (proj_h, proj), (nproj_h, nproj), (tproj_h, tproj), (tpts_h, tpts), (near_h, near), (far_h, far),
             (node_h, node), (nearn_h, nearn), (farn_h, farn), (noden_h, noden)]
    copies = [pltpu.make_async_copy(a, b, sems.at[k]) for k, (a, b) in enumerate(moves)]
    for leaf in range(SL):
        copies.append(pltpu.make_async_copy(idx_h.at[leaf], idx_s.at[pl.ds(LEAF * leaf, LEAF)], sems.at[16 + leaf]))
    for copy in copies:
        copy.start()
    for copy in copies[:5]:
        copy.wait()
    index = idx[...]
    pivots = piv[...]
    node_piv = jnp.broadcast_to(npiv[...], (8, SKEL))
    top_piv = jnp.broadcast_to(tpiv[...], (8, SKEL))
    leaf_of = lax.broadcasted_iota(jnp.int32, (8, 128), 0)
    leaf_c, skel_c, node_c, top_c = [], [], [], []
    for c in range(3):
        chunks = [jnp.broadcast_to(pts[c : c + 1, 128 * k : 128 * (k + 1)], (8, 128)) for k in range(rows // 128)]
        leaf_x = [pick(chunks, lanes(index, m)) for m in range(4)]
        skel_x = [pick(leaf_x, lanes(pivots, m)) for m in range(2)]
        node_x = []
        top_x = []
        for m in range(2):
            at = lanes(node_piv, m)
            mine = jnp.where(leaf_of == (at >> 8), pick(skel_x, at & 255), 0.0)
            node_x.append(jnp.broadcast_to(jnp.sum(mine, axis=0, keepdims=True), (8, 128)))
        for m in range(2):
            at = lanes(top_piv, m)
            top_x.append(jnp.where((at >> 8) == src, centred(pick(node_x, at & 255)), 0.0))
        leaf_c.append(centred(jnp.concatenate(leaf_x, axis=1)))
        skel_c.append(centred(jnp.concatenate(skel_x, axis=1)))
        node_c.append(centred(jnp.concatenate(node_x, axis=1)))
        top_c.append(jnp.concatenate(top_x, axis=1))
    for f, (a, b, n) in enumerate(zip(features(leaf_c, True), features(skel_c, True), features(node_c, True))):
        for leaf in range(SL):
            fs[2 * leaf, f : f + 1, :] = a[leaf : leaf + 1, :256]
            fs[2 * leaf + 1, f : f + 1, :] = a[leaf : leaf + 1, 256:]
            fs[16 + leaf, f : f + 1, :] = b[leaf : leaf + 1, :]
        ns[f : f + 1, :] = n[0:1, :]
    f_out[...] = fs[...].astype(bf16)
    n_out[256:272, :] = ns[:, :128].astype(bf16)
    n_out[272:288, :] = ns[:, 128:].astype(bf16)
    ns[...] = jnp.zeros_like(ns)
    for c in range(3):
        for k, piece in enumerate(split3(top_c[c])):
            ns[3 * c + k : 3 * c + k + 1, :] = piece[0:1, :]
    pieces = ns[...].astype(bf16)
    for copy in copies[9:]:
        copy.wait()
    step = POINT_ROWS // 3
    for c in range(3):
        for k in range(step):
            hf[step * c + k : step * c + k + 1, :] = tpts[c : c + 1, 128 * k : 128 * k + 128]
    for k, piece in enumerate(split3(hf[...])):
        held_out[POINT_ROWS * k : POINT_ROWS * k + POINT_ROWS, :] = piece.astype(bf16)
    lists_out[...] = jnp.zeros_like(lists_out)
    lists_out[NEAR_AT : FAR_AT, :] = near[0]
    for e in range(NODE_AT - FAR_AT):
        lists_out[FAR_AT + e : FAR_AT + e + 1, :] = far[e]
    lists_out[NODE_AT : NEAR_N, :] = node[0]
    lists_out[NEAR_N : NEAR_N + 1, :] = nearn[...]
    lists_out[FAR_N : FAR_N + 1, :] = farn[...]
    lists_out[NODE_N : NODE_N + 1, :] = noden[...]
    lf[...] = jnp.zeros_like(lf)
    lf[:, :TL_J] = lists_out[...].astype(f32)
    held_out[3 * POINT_ROWS :, :] = lf[...].astype(bf16)
    copies[5].wait()

    def widen(k, _):
        at = pl.multiple_of(k * 512, 512)
        wide[pl.ds(at, 512), :] = vals[pl.ds(at, 512), :].astype(f32)
        return 0

    lax.fori_loop(0, rows // 512, widen, 0)

    def gather(k, _):
        at = pl.multiple_of(k * 64, 64)
        for r in range(64):
            gathered[pl.ds(at + r, 1), :] = wide[pl.ds(idx_s[at + r], 1), :]
        return 0

    lax.fori_loop(0, rows // 64, gather, 0)
    for copy in copies[6:9]:
        copy.wait()

    for leaf in range(SL):
        leaf_vals = gathered[leaf * LEAF : (leaf + 1) * LEAF, :].astype(bf16)
        v_out[2 * leaf] = leaf_vals[:256]
        v_out[2 * leaf + 1] = leaf_vals[256:]
        v_out[16 + leaf] = jnp.dot(proj[leaf], leaf_vals, preferred_element_type=f32).astype(bf16)
    node_vals = jnp.dot(
        nproj[0], v_out[16:24].reshape(SL * SKEL, Q), preferred_element_type=f32
    ).astype(bf16)
    n_out[0:256, :] = node_vals
    top = jnp.dot(tproj[0], node_vals, preferred_element_type=f32).T

    for half in range(2):
        for x in range(4):
            part = top[32 * x : 32 * x + 32, 128 * half : 128 * half + 128]
            at = (x - chip) & 3
            t_out[at, 48 * half : 48 * half + 32, :] = part.astype(bf16)
            t_out[at, 48 * half + 32 : 48 * half + 48, :] = lanes(pieces, half)


def target_rows(held, base, hf, first, count, fa):
    step = TL_J * TLEAF // 128
    pieces = [held[base + POINT_ROWS * k : base + POINT_ROWS * (k + 1), :].astype(f32) for k in range(3)]
    hf[...] = pieces[0] + pieces[1] + pieces[2]
    rows = features([centred(hf[pl.ds(step * c + first, count), :]) for c in range(3)], False)
    for f, row in enumerate(rows):
        for k in range(count):
            fa[f : f + 1, 128 * k : 128 * k + 128] = row[k : k + 1, :]


def set_targets(fa, a_ref, count):
    for t in range(count):
        a_ref[t] = fa[:, TLEAF * t : TLEAF * t + TLEAF].T.astype(bf16)
    a_ref[count] = jnp.zeros((TLEAF, KF), bf16)


def run_pairs(pairs, n, trash, a_ref, f_ref, v_of, acc):
    for r in range(TAIL - 1):
        pairs[n + r] = trash

    def group(first, size):
        for q in range(size):
            pair = pairs[first + q]
            s = pair >> 5
            t = pair & 31
            w = jnp.dot(a_ref[t], f_ref[s], preferred_element_type=f32)
            acc[t] += jnp.dot(matern(w), v_of(s), preferred_element_type=f32)

    def large(g, _):
        group(g * GROUP, GROUP)
        return 0

    def small(g, _):
        group(done + g * TAIL, TAIL)
        return 0

    turns = n // GROUP
    done = turns * GROUP
    lax.fori_loop(0, turns, large, 0)
    lax.fori_loop(0, (n - done + TAIL - 1) // TAIL, small, 0)


def leaf_pairs(pairs, lists, start, base, live):
    def target(t, n):
        leaf = start + t
        near, far = live * lists[NEAR_N, leaf], live * lists[FAR_N, leaf]
        for e in range(FAR_AT):
            v = lists[NEAR_AT + e, leaf] - base
            pairs[n] = 64 * v + t
            pairs[n + 1] = 64 * v + 32 + t
            n = n + jnp.where((v >= 0) & (v < SL) & (e < near), 2, 0)
        for e in range(NODE_AT - FAR_AT):
            v = lists[FAR_AT + e, leaf] - base
            pairs[n] = 512 + 32 * v + t
            n = n + jnp.where((v >= 0) & (v < SL) & (e < far), 1, 0)
        return n

    return lax.fori_loop(0, WIN, target, 0)


def clear(acc):
    def one(t, _):
        acc[t] = jnp.zeros(acc.shape[1:], f32)
        return 0

    lax.fori_loop(0, acc.shape[0], one, 0)


def halo_kernel(base, lists, held, v_ref, f_ref, after, out, hf, fa, a_ref, acc, pairs):
    _, _, _, tgt, start = place()
    live = (tgt > 0 if base else tgt < 15).astype(jnp.int32)
    clear(acc)
    target_rows(held, PART, hf, 2 * start, 2 * WIN, fa)
    set_targets(fa, a_ref, WIN)
    n = leaf_pairs(pairs, lists, start, base, live)
    run_pairs(pairs, n, WIN, a_ref, f_ref, lambda s: v_ref[s], acc)
    for t in range(WIN):
        out[t * TLEAF : (t + 1) * TLEAF, :] = acc[t].astype(bf16)


def own_kernel(lists, held, v_ref, f_ref, after, out, a_all, hf, fa, a_ref, pairs):
    start = place()[4]
    clear(out)
    target_rows(held, 0, hf, 0, 2 * TL_J, fa)
    set_targets(fa, a_all, TL_J)
    for t in range(WIN):
        a_ref[t] = a_all[start + t]
    a_ref[WIN] = jnp.zeros((TLEAF, KF), bf16)
    n = leaf_pairs(pairs, lists, start, SL, 1)
    run_pairs(pairs, n, WIN, a_ref, f_ref, lambda s: v_ref[s], out)


def slot_of(column, tgt):
    back = (tgt - column) & 15
    near = back & 3
    far = jnp.where(near == 3, (back >> 2) + 1, back >> 2) & 3
    return 4 * far + near


def node_kernel(
    lists, own, a_ref, halo_l, halo_r, top, y0, y1, y2, y3,
    out, acc, ys, f_ref, pairs, sems,
):
    _, chip, core, tgt, start = place()
    copies = [pltpu.make_async_copy(y, ys.at[k], sems.at[k]) for k, y in enumerate((y0, y1, y2, y3))]
    for copy in copies:
        copy.start()
    clear(acc)
    for t in range(WIN):
        sides = halo_l[t * TLEAF : (t + 1) * TLEAF, :].astype(f32) + halo_r[t * TLEAF : (t + 1) * TLEAF, :].astype(f32)
        acc[start + t] = own[t] + sides

    def target(t, n):
        for e in range(NEAR_N - NODE_AT):
            pairs[n + e] = 32 * slot_of(lists[NODE_AT + e, t], tgt) + t
        return n + lists[NODE_N, t]

    n = lax.fori_loop(0, TL_J, target, 0)
    for copy in copies:
        copy.wait()
    for k in range(4):
        for z in range(4):
            f_ref[4 * k + z, :, 0:128] = ys[k, z * PART + 256 : z * PART + 272, :]
            f_ref[4 * k + z, :, 128:256] = ys[k, z * PART + 272 : z * PART + 288, :]

    def node_vals(s):
        return ys[s >> 2, pl.ds(pl.multiple_of((s & 3) * PART, 32), SKEL), :]

    run_pairs(pairs, n, TRASH, a_ref, f_ref, node_vals, acc)

    def turn(t, _):
        at = pl.multiple_of(t * TLEAF, TLEAF)
        block = acc[t].T
        for x in range(4):
            for k in range(2):
                begin = 16 * (2 * x + k)
                out[k ^ core, (x - chip) & 3, :, pl.ds(at, TLEAF)] = block[begin : begin + 16]
        return 0

    lax.fori_loop(0, TL_J, turn, 0)
    for t in range(TL_J // 2):
        at = pl.multiple_of((core * (TL_J // 2) + t) * TLEAF, TLEAF)
        for k in range(2):
            out[k, 0, :, pl.ds(at, TLEAF)] += top[k, :, t * TLEAF : (t + 1) * TLEAF]


def top_pairs(pairs, listed, counts, tgt, first, count):
    def target(t, n):
        for e in range(listed.shape[1]):
            pairs[n + e] = 32 * slot_of(listed[first + t, e], tgt) + t
        return n + counts[first + t]

    return lax.fori_loop(0, count, target, 0)


def top_kernel(listed, counts, a_all, y0, y1, y2, y3, out, f_ref, v_ref, a_ref, acc, pw, fw, pairs):
    count = TL_J // 2
    _, _, core, tgt, _ = place()
    first = core * count
    for dy, ys in enumerate((y0, y1, y2, y3)):
        for dz in range(4):
            slot = 4 * dy + dz
            for half in range(2):
                at = dz * PART + 288 + 48 * half
                vals = ys[at : at + 32, :].astype(f32)
                v_ref[slot, 128 * half : 128 * half + 128, :] = vals.T.astype(bf16)
                pieces = ys[at + 32 : at + 48, :].astype(f32)
                line = 2 * slot + half
                for p in range(9):
                    pw[p, line : line + 1, :] = pieces[p : p + 1]
    coords = [pw[3 * c] + pw[3 * c + 1] + pw[3 * c + 2] for c in range(3)]
    for f, lines in enumerate(features(coords, True)):
        for line in range(32):
            half = line % 2
            fw[line // 2, f : f + 1, 128 * half : 128 * half + 128] = lines[line : line + 1, :]
    f_ref[...] = fw[...].astype(bf16)
    for t in range(count):
        a_ref[t] = a_all[first + t]
    a_ref[count] = jnp.zeros((TLEAF, KF), bf16)
    clear(acc)
    n = top_pairs(pairs, listed, counts, tgt, first, count)
    run_pairs(pairs, n, count, a_ref, f_ref, lambda s: v_ref[s], acc)
    for t in range(count):
        block = acc[t].T
        for k in range(2):
            out[k ^ core, :, t * TLEAF : (t + 1) * TLEAF] = block[16 * k : 16 * k + 16]


def whole(count):
    return [pl.BlockSpec(memory_space=VMEM)] * count


def params(mebibytes):
    return pltpu.CompilerParams(vmem_limit_bytes=mebibytes << 20)


def cost(flops, moved):
    return pl.CostEstimate(flops=int(flops), bytes_accessed=int(moved), transcendentals=0)


def pair_scratch():
    return [pltpu.SMEM((512,), jnp.int32)]


def shift(axis, count, fn):
    return [(i, fn(i)) for i in range(count) if 0 <= fn(i) < count]


def shards(
    source_points, source_values, leaf_index, leaf_pivots, leaf_proj, node_pivots, node_proj,
    top_pivots, top_proj, target_points, near_list, near_count, far_list, far_count,
    node_list, node_count, top_list, top_count,
):
    smem = pl.BlockSpec(memory_space=SMEM)
    anywhere = pl.BlockSpec(memory_space=pl.ANY)
    v_all, f_all, node_own, top_own, held, lists = pl.pallas_call(
        leaf_kernel,
        out_shape=(
            OUT((24, 256, Q), bf16),
            OUT((24, KF, 256), bf16),
            OUT((288, Q), bf16),
            OUT((4, 96, 128), bf16),
            OUT((HELD, 128), bf16),
            OUT((LIST_ROWS, TL_J), jnp.int32),
        ),
        in_specs=[anywhere] * 16,
        out_specs=tuple(whole(6)),
        scratch_shapes=[
            VMEM((8, 512), jnp.int32),
            VMEM((8, 256), jnp.int32),
            VMEM((1, 256), jnp.int32),
            VMEM((1, 256), jnp.int32),
            VMEM((3, 4096), f32),
            VMEM((4096, Q), bf16),
            VMEM((8, 256, 512), bf16),
            VMEM((1, 256, 2048), bf16),
            VMEM((1, 256, 256), bf16),
            VMEM((3, 4096), f32),
            VMEM((1, 8, TL_J), jnp.int32),
            VMEM((12, 1, TL_J), jnp.int32),
            VMEM((1, 4, TL_J), jnp.int32),
            VMEM((1, TL_J), jnp.int32),
            VMEM((1, TL_J), jnp.int32),
            VMEM((1, TL_J), jnp.int32),
            VMEM((4096, Q), f32),
            VMEM((4096, Q), f32),
            VMEM((24, KF, 256), f32),
            VMEM((KF, 256), f32),
            VMEM((POINT_ROWS, 128), f32),
            VMEM((LIST_ROWS, 128), f32),
            pltpu.SMEM((4096,), jnp.int32),
            pltpu.SemaphoreType.DMA((24,)),
        ],
        compiler_params=params(BIG),
        cost_estimate=cost(8e9, 8e6),
        name="leaf_stage",
    )(leaf_index, leaf_pivots, node_pivots, top_pivots, source_points, source_values,
      leaf_proj, node_proj, top_proj, target_points, near_list.transpose(0, 2, 1), far_list.transpose(2, 0, 1),
      node_list.transpose(0, 2, 1), near_count, far_count, node_count)
    forward = shift("tgt", 16, lambda i: i + 1)
    backward = shift("tgt", 16, lambda i: i - 1)

    around = {d: shift("tgt", 16, lambda i, d=d: (i + d) % 16) for d in (1, -1, 2, 4, 8, 12)}
    yshift = [None, around[4], around[8], around[12]]
    xshift = [shift("src", 8, lambda i, d=d: (i + 2 * d) % 8) for d in range(4)]
    cores = shift("src", 8, lambda i: i ^ 1)

    def others(x, axis, shifts):
        return [lax.ppermute(x, axis, shifts[d]) for d in (1, 3, 2)]

    def in_order(x, got):
        return [x, got[0], got[2], got[1]]

    top_pair = top_own.astype(f32) + lax.ppermute(top_own, "src", cores).astype(f32)
    top_sum = top_pair[0]
    for d in (1, 3, 2):
        top_sum = top_sum + lax.ppermute(top_pair[d].astype(bf16), "src", xshift[d]).astype(f32)
    parts = jnp.concatenate([node_own, top_sum.astype(bf16)], axis=0)
    wide = jnp.concatenate([parts, held], axis=0)
    from_l = lax.ppermute(wide, "tgt", around[1])
    from_r = lax.ppermute(wide, "tgt", around[-1])
    from_2 = lax.ppermute(parts, "tgt", around[2])
    lists_l = from_l[PART + 3 * POINT_ROWS :, :TL_J].astype(jnp.int32)
    lists_r = from_r[PART + 3 * POINT_ROWS :, :TL_J].astype(jnp.int32)
    bundle = jnp.concatenate([parts, from_l[:PART], from_2, from_r[:PART]], axis=0)
    ys = in_order(bundle, others(bundle, "tgt", yshift))

    def halo(base, lists_of, held_of, after):
        return pl.pallas_call(
            functools.partial(halo_kernel, base),
            out_shape=jax.ShapeDtypeStruct((WIN * TLEAF, Q), bf16),
            in_specs=[smem] + whole(3) + [anywhere],
            out_specs=pl.BlockSpec(memory_space=VMEM),
            scratch_shapes=[
                VMEM((POINT_ROWS, 128), f32),
                VMEM((KF, WIN * TLEAF), f32),
                VMEM((WIN + 1, TLEAF, KF), bf16),
                VMEM((WIN + 1, TLEAF, Q), f32),
            ] + pair_scratch(),
            compiler_params=params(24),
            cost_estimate=cost(HALO_COST, 3e6),
            name="halo_terms",
        )(lists_of, held_of, v_all, f_all, after)

    own, a_all = pl.pallas_call(
        own_kernel,
        out_shape=(
            jax.ShapeDtypeStruct((WIN + 1, TLEAF, Q), f32),
            jax.ShapeDtypeStruct((TL_J + 1, TLEAF, KF), bf16),
        ),
        in_specs=[smem] + whole(3) + [anywhere],
        out_specs=tuple(whole(2)),
        scratch_shapes=[
            VMEM((POINT_ROWS, 128), f32),
            VMEM((KF, TL_J * TLEAF), f32),
            VMEM((WIN + 1, TLEAF, KF), bf16),
        ] + pair_scratch(),
        compiler_params=params(24),
        cost_estimate=cost(OWN_COST, 3e6),
        name="own_terms",
    )(lists, held, v_all, f_all, wide)

    to_l = halo(16, lists_l, from_l, own)
    got_r = lax.ppermute(to_l, "tgt", backward)
    to_r = halo(0, lists_r, from_r, to_l)
    got_l = lax.ppermute(to_r, "tgt", forward)

    half = TL_J // 2
    top_term = pl.pallas_call(
        top_kernel,
        out_shape=jax.ShapeDtypeStruct((2, 16, half * TLEAF), f32),
        in_specs=[smem, smem] + whole(5),
        out_specs=pl.BlockSpec(memory_space=VMEM),
        scratch_shapes=[
            VMEM((16, KF, 256), bf16),
            VMEM((16, 256, 32), bf16),
            VMEM((half + 1, TLEAF, KF), bf16),
            VMEM((half + 1, TLEAF, 32), f32),
            VMEM((9, 32, 128), f32),
            VMEM((16, KF, 256), f32),
        ] + pair_scratch(),
        compiler_params=params(24),
        cost_estimate=cost(TOP_COST, 3e6),
        name="top_terms",
    )(top_list, top_count, a_all, *ys)

    partial = pl.pallas_call(
        node_kernel,
        out_shape=jax.ShapeDtypeStruct((2, 4, 16, TL_J * TLEAF), f32),
        in_specs=[smem] + whole(5) + [anywhere] * 4,
        out_specs=pl.BlockSpec(memory_space=VMEM),
        scratch_shapes=[
            VMEM((TL_J + 1, TLEAF, Q), f32),
            VMEM((4, 4 * PART, Q), bf16),
            VMEM((16, KF, 256), bf16),
        ] + pair_scratch() + [pltpu.SemaphoreType.DMA((4,))],
        compiler_params=params(24),
        cost_estimate=cost(NODE_COST, 3e6),
        name="node_terms",
    )(lists, own, a_all, got_l, got_r, top_term, *ys)

    pair = partial[0] + lax.ppermute(partial[1], "src", cores)
    total = pair[0]
    for d in (1, 3, 2):
        total = total + lax.ppermute(pair[d].astype(bf16), "src", xshift[d]).astype(f32)
    return total.T


def solution(mesh):
    both = ("src", "tgt")
    in_specs = (
        P(None, both), P(both, None), P(both, None), P(both, None), P(both, None, None), P(both, None),
        P(both, None, None), P("tgt", None), P("tgt", None, "src"), P(None, "tgt"), P("src", "tgt", None),
        P("src", "tgt"), P("src", "tgt", None), P("src", "tgt"), P("src", "tgt", None), P("src", "tgt"),
        P("tgt", None), P("tgt"),
    )
    return jax.shard_map(shards, mesh=mesh, in_specs=in_specs, out_specs=P("tgt", "src"), check_vma=False)
```

```python
import functools

import jax
import jax.numpy as jnp
from jax import lax
from jax.experimental import pallas as pl
from jax.experimental.pallas import tpu as pltpu
from jax.sharding import PartitionSpec as P

SL = 8
LEAF = 512
SKEL = 256
Q = 128
TLEAF = 256
TL_J = 16
WIN = 6
KF = 16
LN2 = 0.6931471805599453
SCALE = 2.0
GROUP = 16
TAIL = 4
VMEM = pltpu.VMEM
SMEM = pltpu.SMEM
bf16 = jnp.bfloat16
f32 = jnp.float32
NEAR_AT, FAR_AT, NODE_AT = 0, 8, 20
NEAR_N, FAR_N, NODE_N = 24, 25, 26
LIST_ROWS = 32
POINT_ROWS = 96
HELD = 3 * POINT_ROWS + LIST_ROWS
TRASH = 16
PART = 384
BIG = 60
OUT = pltpu.VMEM
HALO_COST = 1e9
OWN_COST = 5e9
NODE_COST = 6e9
TOP_COST = 6e9


def split2(x):
    high = x.astype(bf16).astype(f32)
    return high, (x - high).astype(bf16).astype(f32)


def split3(x):
    high, rest = split2(x)
    return high, rest, (x - high - rest).astype(bf16).astype(f32)


def centred(x):
    return (x - 1.0) * SCALE


def features(coords, is_source):
    pieces = [split2(c) for c in coords]
    high = [p[0] for p in pieces]
    low = [p[1] for p in pieces]
    norm = sum((h + r) * (h + r) for h, r in pieces)
    norms = list(split3(norm))
    one = jnp.ones_like(norm)
    zero = jnp.zeros_like(norm)
    if is_source:
        high = [-2.0 * h for h in high]
        low = [-2.0 * r for r in low]
        return high + low + high + [one, one, one] + norms + [zero]
    return high + high + low + norms + [one, one, one] + [zero]


def matern(w):
    w = jnp.maximum(w, 1e-12)
    u = w * lax.rsqrt(w)
    return ((1.0 + u) * jnp.exp2(u * (-1.0 / LN2))).astype(bf16)


def take(row, index):
    return jnp.take_along_axis(row, index, axis=1, mode="promise_in_bounds")


def pick(chunks, index):
    low = index & 127
    high = index >> 7
    result = jnp.zeros((8, 128), f32)
    for k, chunk in enumerate(chunks):
        result = jnp.where(high == k, take(chunk, low), result)
    return result


def lanes(x, m):
    return x[:, 128 * m : 128 * (m + 1)]


def place():
    src = lax.axis_index("src")
    tgt = lax.axis_index("tgt")
    start = jnp.clip(2 * src - 2, 0, TL_J - WIN)
    return src, src >> 1, src & 1, tgt, start


def leaf_kernel(
    idx_h, piv_h, npiv_h, tpiv_h, pts_h, vals_h, proj_h, nproj_h, tproj_h,
    tpts_h, near_h, far_h, node_h, nearn_h, farn_h, noden_h,
    v_out, f_out, n_out, t_out, held_out, lists_out, idx, piv, npiv, tpiv, pts, vals, proj, nproj, tproj,
    tpts, near, far, node, nearn, farn, noden, wide, gathered, fs, ns, hf, lf, idx_s, sems,
):
    src, chip, _, _, _ = place()
    rows = vals.shape[0]
    moves = [(pts_h, pts), (idx_h, idx), (piv_h, piv), (npiv_h, npiv), (tpiv_h, tpiv), (vals_h, vals),
             (proj_h, proj), (nproj_h, nproj), (tproj_h, tproj), (tpts_h, tpts), (near_h, near), (far_h, far),
             (node_h, node), (nearn_h, nearn), (farn_h, farn), (noden_h, noden)]
    copies = [pltpu.make_async_copy(a, b, sems.at[k]) for k, (a, b) in enumerate(moves)]
    for leaf in range(SL):
        copies.append(pltpu.make_async_copy(idx_h.at[leaf], idx_s.at[pl.ds(LEAF * leaf, LEAF)], sems.at[16 + leaf]))
    for copy in copies:
        copy.start()
    for copy in copies[:5]:
        copy.wait()
    index = idx[...]
    pivots = piv[...]
    node_piv = jnp.broadcast_to(npiv[...], (8, SKEL))
    top_piv = jnp.broadcast_to(tpiv[...], (8, SKEL))
    leaf_of = lax.broadcasted_iota(jnp.int32, (8, 128), 0)
    leaf_c, skel_c, node_c, top_c = [], [], [], []
    for c in range(3):
        chunks = [jnp.broadcast_to(pts[c : c + 1, 128 * k : 128 * (k + 1)], (8, 128)) for k in range(rows // 128)]
        leaf_x = [pick(chunks, lanes(index, m)) for m in range(4)]
        skel_x = [pick(leaf_x, lanes(pivots, m)) for m in range(2)]
        node_x = []
        top_x = []
        for m in range(2):
            at = lanes(node_piv, m)
            mine = jnp.where(leaf_of == (at >> 8), pick(skel_x, at & 255), 0.0)
            node_x.append(jnp.broadcast_to(jnp.sum(mine, axis=0, keepdims=True), (8, 128)))
        for m in range(2):
            at = lanes(top_piv, m)
            top_x.append(jnp.where((at >> 8) == src, centred(pick(node_x, at & 255)), 0.0))
        leaf_c.append(centred(jnp.concatenate(leaf_x, axis=1)))
        skel_c.append(centred(jnp.concatenate(skel_x, axis=1)))
        node_c.append(centred(jnp.concatenate(node_x, axis=1)))
        top_c.append(jnp.concatenate(top_x, axis=1))
    for f, (a, b, n) in enumerate(zip(features(leaf_c, True), features(skel_c, True), features(node_c, True))):
        for leaf in range(SL):
            fs[2 * leaf, f : f + 1, :] = a[leaf : leaf + 1, :256]
            fs[2 * leaf + 1, f : f + 1, :] = a[leaf : leaf + 1, 256:]
            fs[16 + leaf, f : f + 1, :] = b[leaf : leaf + 1, :]
        ns[f : f + 1, :] = n[0:1, :]
    f_out[...] = fs[...].astype(bf16)
    n_out[256:272, :] = ns[:, :128].astype(bf16)
    n_out[272:288, :] = ns[:, 128:].astype(bf16)
    ns[...] = jnp.zeros_like(ns)
    for c in range(3):
        for k, piece in enumerate(split3(top_c[c])):
            ns[3 * c + k : 3 * c + k + 1, :] = piece[0:1, :]
    pieces = ns[...].astype(bf16)
    for copy in copies[9:]:
        copy.wait()
    step = POINT_ROWS // 3
    for c in range(3):
        for k in range(step):
            hf[step * c + k : step * c + k + 1, :] = tpts[c : c + 1, 128 * k : 128 * k + 128]
    for k, piece in enumerate(split3(hf[...])):
        held_out[POINT_ROWS * k : POINT_ROWS * k + POINT_ROWS, :] = piece.astype(bf16)
    lists_out[...] = jnp.zeros_like(lists_out)
    lists_out[NEAR_AT : FAR_AT, :] = near[0]
    for e in range(NODE_AT - FAR_AT):
        lists_out[FAR_AT + e : FAR_AT + e + 1, :] = far[e]
    lists_out[NODE_AT : NEAR_N, :] = node[0]
    lists_out[NEAR_N : NEAR_N + 1, :] = nearn[...]
    lists_out[FAR_N : FAR_N + 1, :] = farn[...]
    lists_out[NODE_N : NODE_N + 1, :] = noden[...]
    lf[...] = jnp.zeros_like(lf)
    lf[:, :TL_J] = lists_out[...].astype(f32)
    held_out[3 * POINT_ROWS :, :] = lf[...].astype(bf16)
    copies[5].wait()

    def widen(k, _):
        at = pl.multiple_of(k * 512, 512)
        wide[pl.ds(at, 512), :] = vals[pl.ds(at, 512), :].astype(f32)
        return 0

    lax.fori_loop(0, rows // 512, widen, 0)

    for copy in copies[6:9]:
        copy.wait()

    def project(leaf):
        at = pl.multiple_of(leaf * LEAF, LEAF)
        leaf_vals = gathered[pl.ds(at, LEAF), :].astype(bf16)
        v_out[2 * leaf] = leaf_vals[:256]
        v_out[2 * leaf + 1] = leaf_vals[256:]
        v_out[16 + leaf] = jnp.dot(proj[leaf], leaf_vals, preferred_element_type=f32).astype(bf16)

    def gather(leaf, _):
        project(jnp.maximum(leaf - 1, 0))
        at = pl.multiple_of(leaf * LEAF, LEAF)
        for r in range(LEAF):
            gathered[pl.ds(at + r, 1), :] = wide[pl.ds(idx_s[at + r], 1), :]
        return 0

    gathered[0:LEAF, :] = jnp.zeros((LEAF, Q), f32)
    lax.fori_loop(0, SL, gather, 0)
    project(SL - 1)
    node_vals = jnp.dot(
        nproj[0], v_out[16:24].reshape(SL * SKEL, Q), preferred_element_type=f32
    ).astype(bf16)
    n_out[0:256, :] = node_vals
    top = jnp.dot(tproj[0], node_vals, preferred_element_type=f32).T

    for half in range(2):
        for x in range(4):
            part = top[32 * x : 32 * x + 32, 128 * half : 128 * half + 128]
            at = (x - chip) & 3
            t_out[at, 48 * half : 48 * half + 32, :] = part.astype(bf16)
            t_out[at, 48 * half + 32 : 48 * half + 48, :] = lanes(pieces, half)


def target_rows(held, base, hf, first, count, fa):
    step = TL_J * TLEAF // 128
    pieces = [held[base + POINT_ROWS * k : base + POINT_ROWS * (k + 1), :].astype(f32) for k in range(3)]
    hf[...] = pieces[0] + pieces[1] + pieces[2]
    rows = features([centred(hf[pl.ds(step * c + first, count), :]) for c in range(3)], False)
    for f, row in enumerate(rows):
        for k in range(count):
            fa[f : f + 1, 128 * k : 128 * k + 128] = row[k : k + 1, :]


def set_targets(fa, a_ref, count):
    for t in range(count):
        a_ref[t] = fa[:, TLEAF * t : TLEAF * t + TLEAF].T.astype(bf16)
    a_ref[count] = jnp.zeros((TLEAF, KF), bf16)


def run_pairs(pairs, n, trash, a_ref, f_ref, v_of, acc):
    for r in range(TAIL - 1):
        pairs[n + r] = trash

    def group(first, size):
        for q in range(size):
            pair = pairs[first + q]
            s = pair >> 5
            t = pair & 31
            w = jnp.dot(a_ref[t], f_ref[s], preferred_element_type=f32)
            acc[t] += jnp.dot(matern(w), v_of(s), preferred_element_type=f32)

    def large(g, _):
        group(g * GROUP, GROUP)
        return 0

    def small(g, _):
        group(done + g * TAIL, TAIL)
        return 0

    turns = n // GROUP
    done = turns * GROUP
    lax.fori_loop(0, turns, large, 0)
    lax.fori_loop(0, (n - done + TAIL - 1) // TAIL, small, 0)


def leaf_pairs(pairs, lists, start, base, live):
    def target(t, n):
        leaf = start + t
        near, far = live * lists[NEAR_N, leaf], live * lists[FAR_N, leaf]
        for e in range(FAR_AT):
            v = lists[NEAR_AT + e, leaf] - base
            pairs[n] = 64 * v + t
            pairs[n + 1] = 64 * v + 32 + t
            n = n + jnp.where((v >= 0) & (v < SL) & (e < near), 2, 0)
        for e in range(NODE_AT - FAR_AT):
            v = lists[FAR_AT + e, leaf] - base
            pairs[n] = 512 + 32 * v + t
            n = n + jnp.where((v >= 0) & (v < SL) & (e < far), 1, 0)
        return n

    return lax.fori_loop(0, WIN, target, 0)


def clear(acc):
    def one(t, _):
        acc[t] = jnp.zeros(acc.shape[1:], f32)
        return 0

    lax.fori_loop(0, acc.shape[0], one, 0)


def halo_kernel(base, lists, held, v_ref, f_ref, after, out, hf, fa, a_ref, acc, pairs):
    _, _, _, tgt, start = place()
    live = (tgt > 0 if base else tgt < 15).astype(jnp.int32)
    clear(acc)
    target_rows(held, PART, hf, 2 * start, 2 * WIN, fa)
    set_targets(fa, a_ref, WIN)
    n = leaf_pairs(pairs, lists, start, base, live)
    run_pairs(pairs, n, WIN, a_ref, f_ref, lambda s: v_ref[s], acc)
    for t in range(WIN):
        out[t * TLEAF : (t + 1) * TLEAF, :] = acc[t].astype(bf16)


def own_kernel(lists, held, v_ref, f_ref, after, out, a_all, hf, fa, a_ref, pairs):
    start = place()[4]
    clear(out)
    target_rows(held, 0, hf, 0, 2 * TL_J, fa)
    set_targets(fa, a_all, TL_J)
    for t in range(WIN):
        a_ref[t] = a_all[start + t]
    a_ref[WIN] = jnp.zeros((TLEAF, KF), bf16)
    n = leaf_pairs(pairs, lists, start, SL, 1)
    run_pairs(pairs, n, WIN, a_ref, f_ref, lambda s: v_ref[s], out)


def slot_of(column, tgt):
    back = (tgt - column) & 15
    near = back & 3
    far = jnp.where(near == 3, (back >> 2) + 1, back >> 2) & 3
    return 4 * far + near


def node_kernel(
    lists, own, a_ref, halo_l, halo_r, top, y0, y1, y2, y3,
    out, acc, ys, f_ref, pairs, sems,
):
    _, chip, core, tgt, start = place()
    copies = [pltpu.make_async_copy(y, ys.at[k], sems.at[k]) for k, y in enumerate((y0, y1, y2, y3))]
    for copy in copies:
        copy.start()
    clear(acc)
    for t in range(WIN):
        sides = halo_l[t * TLEAF : (t + 1) * TLEAF, :].astype(f32) + halo_r[t * TLEAF : (t + 1) * TLEAF, :].astype(f32)
        acc[start + t] = own[t] + sides

    def target(t, n):
        for e in range(NEAR_N - NODE_AT):
            pairs[n + e] = 32 * slot_of(lists[NODE_AT + e, t], tgt) + t
        return n + lists[NODE_N, t]

    n = lax.fori_loop(0, TL_J, target, 0)
    for copy in copies:
        copy.wait()
    for k in range(4):
        for z in range(4):
            f_ref[4 * k + z, :, 0:128] = ys[k, z * PART + 256 : z * PART + 272, :]
            f_ref[4 * k + z, :, 128:256] = ys[k, z * PART + 272 : z * PART + 288, :]

    def node_vals(s):
        return ys[s >> 2, pl.ds(pl.multiple_of((s & 3) * PART, 32), SKEL), :]

    run_pairs(pairs, n, TRASH, a_ref, f_ref, node_vals, acc)

    def turn(t, _):
        at = pl.multiple_of(t * TLEAF, TLEAF)
        block = acc[t].T
        for x in range(4):
            for k in range(2):
                begin = 16 * (2 * x + k)
                out[k ^ core, (x - chip) & 3, :, pl.ds(at, TLEAF)] = block[begin : begin + 16]
        return 0

    lax.fori_loop(0, TL_J, turn, 0)
    for t in range(TL_J // 2):
        at = pl.multiple_of((core * (TL_J // 2) + t) * TLEAF, TLEAF)
        for k in range(2):
            out[k, 0, :, pl.ds(at, TLEAF)] += top[k, :, t * TLEAF : (t + 1) * TLEAF]


def top_pairs(pairs, listed, counts, tgt, first, count):
    def target(t, n):
        for e in range(listed.shape[1]):
            pairs[n + e] = 32 * slot_of(listed[first + t, e], tgt) + t
        return n + counts[first + t]

    return lax.fori_loop(0, count, target, 0)


def top_kernel(listed, counts, a_all, y0, y1, y2, y3, out, f_ref, v_ref, a_ref, acc, pw, fw, pairs):
    count = TL_J // 2
    _, _, core, tgt, _ = place()
    first = core * count
    for dy, ys in enumerate((y0, y1, y2, y3)):
        for dz in range(4):
            slot = 4 * dy + dz
            for half in range(2):
                at = dz * PART + 288 + 48 * half
                vals = ys[at : at + 32, :].astype(f32)
                v_ref[slot, 128 * half : 128 * half + 128, :] = vals.T.astype(bf16)
                pieces = ys[at + 32 : at + 48, :].astype(f32)
                line = 2 * slot + half
                for p in range(9):
                    pw[p, line : line + 1, :] = pieces[p : p + 1]
    coords = [pw[3 * c] + pw[3 * c + 1] + pw[3 * c + 2] for c in range(3)]
    for f, lines in enumerate(features(coords, True)):
        for line in range(32):
            half = line % 2
            fw[line // 2, f : f + 1, 128 * half : 128 * half + 128] = lines[line : line + 1, :]
    f_ref[...] = fw[...].astype(bf16)
    for t in range(count):
        a_ref[t] = a_all[first + t]
    a_ref[count] = jnp.zeros((TLEAF, KF), bf16)
    clear(acc)
    n = top_pairs(pairs, listed, counts, tgt, first, count)
    run_pairs(pairs, n, count, a_ref, f_ref, lambda s: v_ref[s], acc)
    for t in range(count):
        block = acc[t].T
        for k in range(2):
            out[k ^ core, :, t * TLEAF : (t + 1) * TLEAF] = block[16 * k : 16 * k + 16]


def whole(count):
    return [pl.BlockSpec(memory_space=VMEM)] * count


def params(mebibytes):
    return pltpu.CompilerParams(vmem_limit_bytes=mebibytes << 20)


def cost(flops, moved):
    return pl.CostEstimate(flops=int(flops), bytes_accessed=int(moved), transcendentals=0)


def pair_scratch():
    return [pltpu.SMEM((512,), jnp.int32)]


def shift(axis, count, fn):
    return [(i, fn(i)) for i in range(count) if 0 <= fn(i) < count]


def shards(
    source_points, source_values, leaf_index, leaf_pivots, leaf_proj, node_pivots, node_proj,
    top_pivots, top_proj, target_points, near_list, near_count, far_list, far_count,
    node_list, node_count, top_list, top_count,
):
    smem = pl.BlockSpec(memory_space=SMEM)
    anywhere = pl.BlockSpec(memory_space=pl.ANY)
    v_all, f_all, node_own, top_own, held, lists = pl.pallas_call(
        leaf_kernel,
        out_shape=(
            OUT((24, 256, Q), bf16),
            OUT((24, KF, 256), bf16),
            OUT((288, Q), bf16),
            OUT((4, 96, 128), bf16),
            OUT((HELD, 128), bf16),
            OUT((LIST_ROWS, TL_J), jnp.int32),
        ),
        in_specs=[anywhere] * 16,
        out_specs=tuple(whole(6)),
        scratch_shapes=[
            VMEM((8, 512), jnp.int32),
            VMEM((8, 256), jnp.int32),
            VMEM((1, 256), jnp.int32),
            VMEM((1, 256), jnp.int32),
            VMEM((3, 4096), f32),
            VMEM((4096, Q), bf16),
            VMEM((8, 256, 512), bf16),
            VMEM((1, 256, 2048), bf16),
            VMEM((1, 256, 256), bf16),
            VMEM((3, 4096), f32),
            VMEM((1, 8, TL_J), jnp.int32),
            VMEM((12, 1, TL_J), jnp.int32),
            VMEM((1, 4, TL_J), jnp.int32),
            VMEM((1, TL_J), jnp.int32),
            VMEM((1, TL_J), jnp.int32),
            VMEM((1, TL_J), jnp.int32),
            VMEM((4096, Q), f32),
            VMEM((4096, Q), f32),
            VMEM((24, KF, 256), f32),
            VMEM((KF, 256), f32),
            VMEM((POINT_ROWS, 128), f32),
            VMEM((LIST_ROWS, 128), f32),
            pltpu.SMEM((4096,), jnp.int32),
            pltpu.SemaphoreType.DMA((24,)),
        ],
        compiler_params=params(BIG),
        cost_estimate=cost(8e9, 8e6),
        name="leaf_stage",
    )(leaf_index, leaf_pivots, node_pivots, top_pivots, source_points, source_values,
      leaf_proj, node_proj, top_proj, target_points, near_list.transpose(0, 2, 1), far_list.transpose(2, 0, 1),
      node_list.transpose(0, 2, 1), near_count, far_count, node_count)
    forward = shift("tgt", 16, lambda i: i + 1)
    backward = shift("tgt", 16, lambda i: i - 1)

    around = {d: shift("tgt", 16, lambda i, d=d: (i + d) % 16) for d in (1, -1, 2, 4, 8, 12)}
    yshift = [None, around[4], around[8], around[12]]
    xshift = [shift("src", 8, lambda i, d=d: (i + 2 * d) % 8) for d in range(4)]
    cores = shift("src", 8, lambda i: i ^ 1)

    def others(x, axis, shifts):
        return [lax.ppermute(x, axis, shifts[d]) for d in (1, 3, 2)]

    def in_order(x, got):
        return [x, got[0], got[2], got[1]]

    top_pair = top_own.astype(f32) + lax.ppermute(top_own, "src", cores).astype(f32)
    top_sum = top_pair[0]
    for d in (1, 3, 2):
        top_sum = top_sum + lax.ppermute(top_pair[d].astype(bf16), "src", xshift[d]).astype(f32)
    parts = jnp.concatenate([node_own, top_sum.astype(bf16)], axis=0)
    wide = jnp.concatenate([parts, held], axis=0)
    from_l = lax.ppermute(wide, "tgt", around[1])
    from_r = lax.ppermute(wide, "tgt", around[-1])
    from_2 = lax.ppermute(parts, "tgt", around[2])
    lists_l = from_l[PART + 3 * POINT_ROWS :, :TL_J].astype(jnp.int32)
    lists_r = from_r[PART + 3 * POINT_ROWS :, :TL_J].astype(jnp.int32)
    bundle = jnp.concatenate([parts, from_l[:PART], from_2, from_r[:PART]], axis=0)
    ys = in_order(bundle, others(bundle, "tgt", yshift))

    def halo(base, lists_of, held_of, after):
        return pl.pallas_call(
            functools.partial(halo_kernel, base),
            out_shape=jax.ShapeDtypeStruct((WIN * TLEAF, Q), bf16),
            in_specs=[smem] + whole(3) + [anywhere],
            out_specs=pl.BlockSpec(memory_space=VMEM),
            scratch_shapes=[
                VMEM((POINT_ROWS, 128), f32),
                VMEM((KF, WIN * TLEAF), f32),
                VMEM((WIN + 1, TLEAF, KF), bf16),
                VMEM((WIN + 1, TLEAF, Q), f32),
            ] + pair_scratch(),
            compiler_params=params(24),
            cost_estimate=cost(HALO_COST, 3e6),
            name="halo_terms",
        )(lists_of, held_of, v_all, f_all, after)

    own, a_all = pl.pallas_call(
        own_kernel,
        out_shape=(
            jax.ShapeDtypeStruct((WIN + 1, TLEAF, Q), f32),
            jax.ShapeDtypeStruct((TL_J + 1, TLEAF, KF), bf16),
        ),
        in_specs=[smem] + whole(3) + [anywhere],
        out_specs=tuple(whole(2)),
        scratch_shapes=[
            VMEM((POINT_ROWS, 128), f32),
            VMEM((KF, TL_J * TLEAF), f32),
            VMEM((WIN + 1, TLEAF, KF), bf16),
        ] + pair_scratch(),
        compiler_params=params(24),
        cost_estimate=cost(OWN_COST, 3e6),
        name="own_terms",
    )(lists, held, v_all, f_all, wide)

    to_l = halo(16, lists_l, from_l, own)
    got_r = lax.ppermute(to_l, "tgt", backward)
    to_r = halo(0, lists_r, from_r, to_l)
    got_l = lax.ppermute(to_r, "tgt", forward)

    half = TL_J // 2
    top_term = pl.pallas_call(
        top_kernel,
        out_shape=jax.ShapeDtypeStruct((2, 16, half * TLEAF), f32),
        in_specs=[smem, smem] + whole(5),
        out_specs=pl.BlockSpec(memory_space=VMEM),
        scratch_shapes=[
            VMEM((16, KF, 256), bf16),
            VMEM((16, 256, 32), bf16),
            VMEM((half + 1, TLEAF, KF), bf16),
            VMEM((half + 1, TLEAF, 32), f32),
            VMEM((9, 32, 128), f32),
            VMEM((16, KF, 256), f32),
        ] + pair_scratch(),
        compiler_params=params(24),
        cost_estimate=cost(TOP_COST, 3e6),
        name="top_terms",
    )(top_list, top_count, a_all, *ys)

    partial = pl.pallas_call(
        node_kernel,
        out_shape=jax.ShapeDtypeStruct((2, 4, 16, TL_J * TLEAF), f32),
        in_specs=[smem] + whole(5) + [anywhere] * 4,
        out_specs=pl.BlockSpec(memory_space=VMEM),
        scratch_shapes=[
            VMEM((TL_J + 1, TLEAF, Q), f32),
            VMEM((4, 4 * PART, Q), bf16),
            VMEM((16, KF, 256), bf16),
        ] + pair_scratch() + [pltpu.SemaphoreType.DMA((4,))],
        compiler_params=params(24),
        cost_estimate=cost(NODE_COST, 3e6),
        name="node_terms",
    )(lists, own, a_all, got_l, got_r, top_term, *ys)

    pair = partial[0] + lax.ppermute(partial[1], "src", cores)
    total = pair[0]
    for d in (1, 3, 2):
        total = total + lax.ppermute(pair[d].astype(bf16), "src", xshift[d]).astype(f32)
    return total.T


def solution(mesh):
    both = ("src", "tgt")
    in_specs = (
        P(None, both), P(both, None), P(both, None), P(both, None), P(both, None, None), P(both, None),
        P(both, None, None), P("tgt", None), P("tgt", None, "src"), P(None, "tgt"), P("src", "tgt", None),
        P("src", "tgt"), P("src", "tgt", None), P("src", "tgt"), P("src", "tgt", None), P("src", "tgt"),
        P("tgt", None), P("tgt"),
    )
    return jax.shard_map(shards, mesh=mesh, in_specs=in_specs, out_specs=P("tgt", "src"), check_vma=False)
```
